768 devices in a mesh: fsdp: 24 (over z_lo, x), tp: 32 (over z_hi, y, core).
Axes of the slice: x: 4, y: 8, z: 12 (z_hi: 2, z_lo: 6; z = z_hi * 6 + z_lo), core: 2. Of those that a mesh axis runs over, the one named last changes fastest.
Arguments:
- codes: bfloat16 [15360, 8192], P('fsdp', 'tp'), may hold values from -448 to 448, as said below
- offsets: int32 [120, 64], P('fsdp', 'tp'), may hold values from -8 to -4
- responses: bfloat16 [6144, 15360], P('fsdp'), may hold values from -6 to 6
- head: bfloat16 [8192], P('tp'), may hold values from -0.0625 to 0.0625
Outputs:
- projected_out: bfloat16 [6144, 8192], P('fsdp', 'tp')
- scores: float32 [6144], P('fsdp')
The draws below stay inside these ranges and needn't reach their ends.
Inputs may be any that keep to these rules, and one draw needn't show every extreme that they name: `codes`: code values held in bfloat16.
All inputs are finite; a program needn't handle non-finite values.
Results may differ from the reference program's by a relative error of at most 0.0034.
Values may be sent and summed in bfloat16 or wider, within the bound.
A program may use at most 64 MiB of HBM per device.

```python
import jax
import jax.numpy as jnp
from jax import lax

BLK = 128
D = 8192
FFW = 15360
RESPONSES = 6144


def shared_pattern(key):
    picked = jax.random.bernoulli(jax.random.fold_in(key, 5), 0.5, (FFW,))
    return jnp.where(picked, 1.0, -1.0).astype(jnp.float32)


def draw_codes(key, part):
    pattern = shared_pattern(key)
    key = jax.random.fold_in(key, 11)
    key_base, key_rows, key_cols, key_blocks, key_signs = jax.random.split(key, 5)
    base_values = jax.random.uniform(key_base, (FFW, D), jnp.float32, -1.0, 1.0)
    column_pick = jax.random.bernoulli(key_signs, 0.5, (D,))
    column_signs = jnp.where(column_pick, 1.0, -1.0).astype(jnp.float32)
    mixed = jnp.clip(base_values + 0.035 * pattern[:, None] * column_signs[None, :], -1.0, 1.0)
    row_factor = jnp.exp(jax.random.uniform(key_rows, (FFW, 1), jnp.float32, jnp.log(0.1), 0.0))
    col_factor = jnp.exp(jax.random.uniform(key_cols, (1, D), jnp.float32, jnp.log(0.1), 0.0))
    block_factor = jnp.exp(jax.random.uniform(key_blocks, (FFW // BLK, 1, D // BLK, 1), jnp.float32, jnp.log(0.05), 0.0))
    spread = jnp.broadcast_to(block_factor, (FFW // BLK, BLK, D // BLK, BLK)).reshape(FFW, D)
    values = 448.0 * mixed * row_factor * col_factor * spread
    return values.astype(jnp.bfloat16)


def draw_responses(key, part):
    pattern = shared_pattern(key)
    key = jax.random.fold_in(key, 23)
    key_noise = jax.random.fold_in(key, 0)
    key_strength = jax.random.fold_in(key, 1)
    key_signs = jax.random.fold_in(key, 3)
    noise = jnp.clip(jax.random.normal(key_noise, (RESPONSES, FFW), jnp.float32), -4.5, 4.5)
    strength = jax.random.uniform(key_strength, (RESPONSES, 1), jnp.float32, 0.4, 1.0)
    row_pick = jax.random.bernoulli(key_signs, 0.5, (RESPONSES, 1))
    row_signs = jnp.where(row_pick, 1.0, -1.0).astype(jnp.float32)
    values = noise + strength * row_signs * pattern[None, :]
    return values.astype(jnp.bfloat16)


def plant(values, stream_key, low, largest):
    longest = values.shape.index(max(values.shape))
    spots = []
    for shift in (0, 1):
        where = [jax.random.randint(jax.random.fold_in(stream_key, axis), (), 0, length) for axis, length in enumerate(values.shape)]
        where[longest] = (where[longest] + shift) % values.shape[longest]
        spots.append(tuple(where))
    return values.at[spots[0]].set(low).at[spots[1]].set(largest)


def shard_levels(rng, shape, shards, least, high):
    factor_of = 1.0
    for axis_at, shards_of in shards:
        draws = jax.random.uniform(jax.random.fold_in(jax.random.fold_in(rng, 6), axis_at), (shards_of,), jnp.float32, least / len(shards), high / len(shards))
        factor_of = factor_of * jnp.repeat(jnp.exp(draws), shape[axis_at] // shards_of).reshape((-1,) + (1,) * (len(shape) - 1 - axis_at))
    return factor_of


def bell_draw(rng, shape, scale, limit, shards=(), kind=jnp.bfloat16):
    gain = shard_levels(rng, shape, shards, -0.22, 0.18) if shards else 1.0
    drawn = jax.random.normal(rng, shape, jnp.float32) * scale * gain
    return jnp.minimum(jnp.maximum(drawn, -limit), limit).astype(kind)


def setup_inputs(seed: int = 0) -> dict:
    splits = jax.random.split(jax.random.key(seed), 5)
    return {
        "codes": draw_codes(jax.random.fold_in(splits[4], 71), 0),
        "offsets": plant(jax.random.randint(splits[1], (FFW // BLK, D // BLK), -8, -3), jax.random.fold_in(splits[1], 1), -8, (-3) - 1).astype(jnp.int32),
        "responses": draw_responses(jax.random.fold_in(splits[4], 71), 0),
        "head": bell_draw(splits[3], (D,), D ** -0.5, 0.0625, ((0, 32),)),
    }


def block_scales(codes, offsets):
    rows, cols = codes.shape
    blocks = jnp.abs(codes.astype(jnp.float32)).reshape(rows // BLK, BLK, cols // BLK, BLK)
    amax = lax.optimization_barrier(jnp.max(blocks, axis=(1, 3)))
    return jnp.exp2(offsets.astype(jnp.float32)) / (amax + 1e-06)

def dequantize(codes, scales):
    rows, cols = codes.shape
    blocks = codes.astype(jnp.float32).reshape(rows // BLK, BLK, cols // BLK, BLK) * scales[:, None, :, None]
    return blocks.reshape(rows, cols).astype(jnp.bfloat16)

def reference(codes, offsets, responses, head):
    scales = block_scales(codes, offsets)
    weight = dequantize(codes, scales)
    projected = jnp.dot(responses, weight, preferred_element_type=jnp.float32)
    power = lax.optimization_barrier(jnp.sum(projected * projected, axis=1)) / D
    along = lax.optimization_barrier(jnp.sum(projected * head.astype(jnp.float32)[None, :], axis=1))
    scores = along / jnp.sqrt(power + 1e-06)
    return (projected.astype(jnp.bfloat16), scores)
```

```python
import jax
import jax.numpy as jnp
from jax import lax
from jax.experimental import pallas as pl
from jax.experimental.pallas import tpu as pltpu
from jax.sharding import PartitionSpec as P

MESH = pl.DeviceIdType.MESH
BLK = 128
D = 8192
NX, NY, NZ, NH = 4, 8, 6, 3
ROWS = 256
CHUNK = 640
COLS = 256
HALF = NX * NH * CHUNK
SLOTS = NX * NH
ZF = 512
SUB = HALF // 2
PIECE = ROWS // (2 * NY)


def device(x, y, zl, zh, c):
    return (zl * NX + x, (zh * NY + y) * 2 + c)


def kernel(
    codes, offsets, responses, head, out, scores,
    rall, w, acc, pin, s0, s1, ys, z0, z1,
    own_sem, inj_s, inj_r, ring_s, ring_r, sib_s, sib_r,
    wz_s, wz_r, wx_s, wx_r, p_s, p_r, sc_s, sc_r,
):
    f, t = lax.axis_index("fsdp"), lax.axis_index("tp")
    x, zl = f % NX, f // NX
    c, y, zh = t % 2, (t // 2) % NY, t // (2 * NY)
    h, p = zl // NH, zl % NH

    sibling = device(x, y, zl, zh, 1 - c)

    def at_x(e):
        return device((x + e) % NX, y, zl, zh, c)

    def at_z(e):
        return device(x, y, h * NH + (p + e) % NH, zh, c)

    def at_y(e):
        return device(x, (y + e + NY) % NY, zl, zh, c)

    z = zh * NZ + zl
    near = jnp.where(zl < 2, z + 10, jnp.where(zl == 2, z + 1, jnp.where(zl == 3, z + 11, z + 2))) % (2 * NZ)
    wants = device(x, y, near % NZ, near // NZ, c)
    mate_zl = jnp.where(zl < 2, zl + 4, jnp.where(zl == 2, 3, jnp.where(zl == 3, 2, zl - 4)))
    mate = device(x, y, mate_zl, zh, c)
    other = device(x, y, zl, 1 - zh, c)

    barrier = pltpu.get_barrier_semaphore()
    partners = [sibling, wants, mate, other]
    partners += [at_x(e) for e in range(1, NX)]
    partners += [at_z(e) for e in range(1, NH)]
    partners += [at_y(e) for e in range(1, NY)]
    for partner in partners:
        pl.semaphore_signal(barrier, inc=1, device_id=partner, device_id_type=MESH)

    own = pltpu.make_async_copy(
        responses.at[:, pl.ds(pl.multiple_of(h * HALF, 128), HALF)],
        rall.at[pl.ds(0, ROWS)],
        own_sem,
    )
    own.start()

    def slot(xe, pe):
        return ((p + pe) % NH) * NX + (x + xe) % NX

    mine = slot(0, 0)
    for i in range(CHUNK // BLK):
        for j in range(COLS // BLK):
            block = codes[i * BLK : (i + 1) * BLK, j * BLK : (j + 1) * BLK].astype(jnp.float32)
            amax = jnp.max(jnp.max(jnp.abs(block), axis=0, keepdims=True), axis=1, keepdims=True)
            scale = jnp.exp2(offsets[i : i + 1, j : j + 1].astype(jnp.float32)) / (amax + 1e-06)
            w[mine, i * BLK : (i + 1) * BLK, j * BLK : (j + 1) * BLK] = (block * scale).astype(jnp.bfloat16)

    pl.semaphore_wait(barrier, len(partners))

    sent = []

    def send(src, dst, send_sem, recv_sem, to):
        copy = pltpu.make_async_remote_copy(
            src_ref=src, dst_ref=dst, send_sem=send_sem, recv_sem=recv_sem,
            device_id=to, device_id_type=MESH,
        )
        copy.start()
        sent.append(copy)

    def arrived(dst, send_sem, recv_sem):
        pltpu.make_async_remote_copy(
            src_ref=dst, dst_ref=dst, send_sem=send_sem, recv_sem=recv_sem,
            device_id=sibling, device_id_type=MESH,
        ).wait_recv()

    def piece(yo, core, k):
        row = pl.multiple_of(ROWS + 2 * PIECE * yo + PIECE * core, PIECE)
        return rall.at[pl.ds(row, PIECE), pl.ds(k * SUB, SUB)]

    def zpart(s):
        return w.at[s, pl.ds(0, ZF)]

    def xpart(s):
        return w.at[s, pl.ds(ZF, CHUNK - ZF)]

    count = {"wz": 0, "wx": 0, "ring": 0}

    def send_w(kind, s, to):
        n = count[kind]
        count[kind] += 1
        ref = zpart(s) if kind == "wz" else xpart(s)
        sems, recv = (wz_s, wz_r) if kind == "wz" else (wx_s, wx_r)
        send(ref, ref, sems.at[n], recv.at[s], to)

    for k in range(2):
        row = pl.multiple_of(2 * PIECE * y + PIECE * c, PIECE)
        col = pl.multiple_of((1 - h) * HALF + k * SUB, 128)
        send(
            responses.at[pl.ds(row, PIECE), pl.ds(col, SUB)],
            piece(y, c, k), inj_s.at[k], inj_r.at[k], wants,
        )
    for e in range(1, NX):
        send_w("wx", mine, at_x(e))
    for e in range(1, NH):
        send_w("wz", mine, at_z(e))
    for e in range(1, NX):
        send_w("wz", mine, at_x(e))
    for e in range(1, NH):
        send_w("wx", mine, at_z(e))

    def ring(dir_, k, d):
        yo = (y - dir_ * d + NY) % NY
        ref = piece(yo, c, k)
        last = 4 if (dir_ == 1) == (k == 0) else 3
        i = (0 if dir_ == 1 else 1) * 8 + k * 4
        if d > 0:
            arrived(ref, ring_s.at[i + d - 1], ring_r.at[i + d - 1])
        if d < last:
            send(ref, ref, ring_s.at[i + d], ring_r.at[i + d], at_y(dir_))
        if d > 0 or dir_ == 1:
            n = count["ring"]
            count["ring"] += 1
            send(ref, ref, sib_s.at[n], sib_r.at[n], sibling)
            sibs.append((yo, k, n))

    sibs = []

    def ring_step(d):
        for k in range(2):
            for dir_ in (1, -1):
                if d <= (4 if (dir_ == 1) == (k == 0) else 3):
                    ring(dir_, k, d)

    def forward_x(xe):
        s = slot(xe, 0)
        arrived(xpart(s), wx_s.at[0], wx_r.at[s])
        for e in range(1, NH):
            send_w("wx", s, at_z(e))

    def forward_z(pe):
        s = slot(0, pe)
        arrived(zpart(s), wz_s.at[0], wz_r.at[s])
        for e in range(1, NX):
            send_w("wz", s, at_x(e))

    for k in range(2):
        arrived(piece(y, c, k), inj_s.at[k], inj_r.at[k])
        ring(1, k, 0)
        ring(-1, k, 0)
    for xe in (1, 3, 2):
        forward_x(xe)
    ring_step(1)
    forward_z(1)
    ring_step(2)
    forward_z(2)
    ring_step(3)
    ring_step(4)
    for yo, k, n in sibs:
        arrived(piece(yo, 1 - c, k), sib_s.at[n], sib_r.at[n])
    own.wait()

    acc[...] = jnp.zeros_like(acc)

    def multiply(i, carry):
        pe, xe = i // NX, i % NX
        s = slot(xe, pe)

        @pl.when(xe != 0)
        def _():
            arrived(zpart(s), wz_s.at[0], wz_r.at[s])

        @pl.when(pe != 0)
        def _():
            arrived(xpart(s), wx_s.at[0], wx_r.at[s])

        cols = pl.ds(pl.multiple_of(s * CHUNK, 128), CHUNK)
        acc[...] += jnp.dot(rall[:, cols], w[s], preferred_element_type=jnp.float32)
        return carry

    lax.fori_loop(0, SLOTS, multiply, 0)

    send(acc.at[pl.ds(ROWS, ROWS)], pin, p_s, p_r, mate)
    arrived(pin, p_s, p_r)
    projected = acc[0:ROWS] + pin[...]
    out[...] = projected.astype(out.dtype)

    def over_columns(v):
        return jnp.sum((v[:, :128] + v[:, 128:]).T, axis=0, keepdims=True)

    s0[...] = jnp.zeros_like(s0)
    s0[0:1] = over_columns(projected * projected)
    s0[1:2] = over_columns(projected * head[...].astype(jnp.float32))
    send(s0, s1, sc_s.at[0], sc_r.at[0], sibling)
    arrived(s1, sc_s.at[0], sc_r.at[0])
    ys[y] = s0[...] + s1[...]
    for e in range(1, NY):
        send(ys.at[y], ys.at[y], sc_s.at[e], sc_r.at[e], at_y(e))
    for e in range(1, NY):
        arrived(ys.at[(y - e + NY) % NY], sc_s.at[e], sc_r.at[e])
    z0[...] = jnp.sum(ys[...], axis=0)
    send(z0, z1, sc_s.at[NY], sc_r.at[NY], other)
    arrived(z1, sc_s.at[NY], sc_r.at[NY])
    total = z0[...] + z1[...]
    scores[...] = total[1:2] / jnp.sqrt(total[0:1] / D + 1e-06)

    for copy in sent:
        copy.wait_send()


def on_device(codes, offsets, responses, head):
    vmem = pl.BlockSpec(memory_space=pltpu.VMEM)
    dma = pltpu.SemaphoreType.DMA
    f32, bf16 = jnp.float32, jnp.bfloat16
    out, scores = pl.pallas_call(
        kernel,
        out_shape=(
            jax.ShapeDtypeStruct((ROWS, COLS), bf16),
            jax.ShapeDtypeStruct((1, ROWS), f32),
        ),
        in_specs=[vmem, vmem, pl.BlockSpec(memory_space=pl.ANY), vmem],
        out_specs=(vmem, vmem),
        scratch_shapes=[
            pltpu.VMEM((2 * ROWS, HALF), bf16),
            pltpu.VMEM((SLOTS, CHUNK, COLS), bf16),
            pltpu.VMEM((2 * ROWS, COLS), f32),
            pltpu.VMEM((ROWS, COLS), f32),
            pltpu.VMEM((8, ROWS), f32),
            pltpu.VMEM((8, ROWS), f32),
            pltpu.VMEM((NY, 8, ROWS), f32),
            pltpu.VMEM((8, ROWS), f32),
            pltpu.VMEM((8, ROWS), f32),
            dma,
            dma((2,)), dma((2,)),
            dma((16,)), dma((16,)),
            dma((16,)), dma((16,)),
            dma((12,)), dma((SLOTS,)),
            dma((12,)), dma((SLOTS,)),
            dma, dma,
            dma((NY + 1,)), dma((NY + 1,)),
        ],
        compiler_params=pltpu.CompilerParams(
            collective_id=0, has_side_effects=True, vmem_limit_bytes=60 * 2**20
        ),
        cost_estimate=pl.CostEstimate(flops=2 * ROWS * 2 * HALF * COLS, bytes_accessed=8 * 2**20, transcendentals=0),
        name="project_and_score",
    )(codes, offsets, responses, head.reshape(1, COLS))
    return out, scores.reshape(ROWS)


def solution(mesh):
    in_specs = (P("fsdp", "tp"), P("fsdp", "tp"), P("fsdp", None), P("tp"))
    out_specs = (P("fsdp", "tp"), P("fsdp"))
    return jax.shard_map(
        on_device, mesh=mesh, in_specs=in_specs, out_specs=out_specs, check_vma=False
    )
```

```python
import jax
import jax.numpy as jnp
from jax import lax
from jax.experimental import pallas as pl
from jax.experimental.pallas import tpu as pltpu
from jax.sharding import PartitionSpec as P

MESH = pl.DeviceIdType.MESH
BLK = 128
D = 8192
NX, NY, NZ, NH = 4, 8, 6, 3
ROWS = 256
CHUNK = 640
COLS = 256
HALF = NX * NH * CHUNK
SLOTS = NX * NH
ZF = 464
SUB = HALF // 2
PIECE = ROWS // (2 * NY)


def device(x, y, zl, zh, c):
    return (zl * NX + x, (zh * NY + y) * 2 + c)


def kernel(
    codes, offsets, responses, head, out, scores,
    rall, w, acc, pout, pin, kout, kin, s0, s1, ys,
    own_sem, inj_s, inj_r, ring_s, ring_r, sib_s, sib_r,
    wz_s, wz_r, wx_s, wx_r, p_s, p_r, k_s, k_r, sc_s, sc_r,
):
    f, t = lax.axis_index("fsdp"), lax.axis_index("tp")
    x, zl = f % NX, f // NX
    c, y, zh = t % 2, (t // 2) % NY, t // (2 * NY)
    h, p = zl // NH, zl % NH

    sibling = device(x, y, zl, zh, 1 - c)

    def at_x(e):
        return device((x + e) % NX, y, zl, zh, c)

    def at_z(e):
        return device(x, y, h * NH + (p + e) % NH, zh, c)

    def at_y(e):
        return device(x, (y + e + NY) % NY, zl, zh, c)

    mate = device(x, y, NZ - 1 - zl, zh, c)
    outer, middle = (zl == 0) | (zl == NZ - 1), (zl == NH - 1) | (zl == NH)
    wants = [
        device(x, y, NZ - 1 - zl, jnp.where(outer, 1 - zh, zh), c),
        device(x, y, NZ - 1 - zl, jnp.where(middle, zh, 1 - zh), c),
    ]
    group = [(e, g) for g in range(2) for e in range(NY) if e or g]

    def at_group(e, g):
        return device(x, (y + e) % NY, zl, (zh + g) % 2, c)

    barrier = pltpu.get_barrier_semaphore()
    partners = [sibling, mate, *wants]
    partners += [at_x(e) for e in range(1, NX)]
    partners += [at_z(e) for e in range(1, NH)]
    partners += [at_group(e, g) for e, g in group]
    for partner in partners:
        pl.semaphore_signal(barrier, inc=1, device_id=partner, device_id_type=MESH)

    own = pltpu.make_async_copy(
        responses.at[:, pl.ds(pl.multiple_of(h * HALF, 128), HALF)],
        rall.at[pl.ds(0, ROWS)],
        own_sem,
    )
    own.start()

    def slot(xe, pe):
        return ((p + pe) % NH) * NX + (x + xe) % NX

    mine = slot(0, 0)
    for i in range(CHUNK // BLK):
        for j in range(COLS // BLK):
            block = codes[i * BLK : (i + 1) * BLK, j * BLK : (j + 1) * BLK].astype(jnp.float32)
            amax = jnp.max(jnp.max(jnp.abs(block), axis=0, keepdims=True), axis=1, keepdims=True)
            scale = jnp.exp2(offsets[j : j + 1, i : i + 1].astype(jnp.float32)) / (amax + 1e-06)
            w[mine, i * BLK : (i + 1) * BLK, j * BLK : (j + 1) * BLK] = (block * scale).astype(jnp.bfloat16)

    pl.semaphore_wait(barrier, len(partners))

    sent = []

    def send(src, dst, send_sem, recv_sem, to):
        copy = pltpu.make_async_remote_copy(
            src_ref=src, dst_ref=dst, send_sem=send_sem, recv_sem=recv_sem,
            device_id=to, device_id_type=MESH,
        )
        copy.start()
        sent.append(copy)

    def arrived(dst, send_sem, recv_sem):
        pltpu.make_async_remote_copy(
            src_ref=dst, dst_ref=dst, send_sem=send_sem, recv_sem=recv_sem,
            device_id=sibling, device_id_type=MESH,
        ).wait_recv()

    def piece(yo, core, k):
        row = pl.multiple_of(ROWS + 2 * PIECE * yo + PIECE * core, PIECE)
        return rall.at[pl.ds(row, PIECE), pl.ds(k * SUB, SUB)]

    def zpart(s):
        return w.at[s, pl.ds(0, ZF)]

    def xpart(s):
        return w.at[s, pl.ds(ZF, CHUNK - ZF)]

    count = {"wz": 0, "wx": 0, "ring": 0}

    def send_w(kind, s, to):
        n = count[kind]
        count[kind] += 1
        ref = zpart(s) if kind == "wz" else xpart(s)
        sems, recv = (wz_s, wz_r) if kind == "wz" else (wx_s, wx_r)
        send(ref, ref, sems.at[n], recv.at[s], to)

    for k in range(2):
        row = pl.multiple_of(2 * PIECE * y + PIECE * c, PIECE)
        col = pl.multiple_of((1 - h) * HALF + k * SUB, 128)
        send(
            responses.at[pl.ds(row, PIECE), pl.ds(col, SUB)],
            piece(y, c, k), inj_s.at[k], inj_r.at[k], wants[k],
        )
    first = jnp.where(p == NH - 1, 2, 1)
    for e in (1, 3, 2):
        send_w("wx", mine, at_x(e))
    for e in (first, NH - first):
        send_w("wz", mine, at_z(e))
    for e in (1, 3, 2):
        send_w("wz", mine, at_x(e))
    for e in (first, NH - first):
        send_w("wx", mine, at_z(e))

    def ring(dir_, k, d):
        yo = (y - dir_ * d + NY) % NY
        ref = piece(yo, c, k)
        last = 4 if (dir_ == 1) == (k == 0) else 3
        i = (0 if dir_ == 1 else 1) * 8 + k * 4
        if d > 0:
            arrived(ref, ring_s.at[i + d - 1], ring_r.at[i + d - 1])
        if d < last:
            send(ref, ref, ring_s.at[i + d], ring_r.at[i + d], at_y(dir_))
        if d > 0 or dir_ == 1:
            n = count["ring"]
            count["ring"] += 1
            send(ref, ref, sib_s.at[n], sib_r.at[n], sibling)
            sibs.append((yo, k, n))

    sibs = []

    def ring_step(d, k):
        for dir_ in (1, -1):
            if d <= (4 if (dir_ == 1) == (k == 0) else 3):
                ring(dir_, k, d)

    def forward_x(xe):
        s = slot(xe, 0)
        arrived(xpart(s), wx_s.at[0], wx_r.at[s])
        for e in (first, NH - first):
            send_w("wx", s, at_z(e))

    def forward_z(pe):
        s = slot(0, pe)
        arrived(zpart(s), wz_s.at[0], wz_r.at[s])
        for e in (1, 3, 2):
            send_w("wz", s, at_x(e))

    def ring_start(k):
        arrived(piece(y, c, k), inj_s.at[k], inj_r.at[k])
        ring(1, k, 0)
        ring(-1, k, 0)

    ring_start(0)
    for xe in (1, 3, 2):
        forward_x(xe)
    ring_start(1)
    ring_step(1, 0)
    forward_z(first)
    ring_step(1, 1)
    ring_step(2, 0)
    forward_z(NH - first)
    ring_step(2, 1)
    for d in (3, 4):
        for k in range(2):
            ring_step(d, k)
    for yo, k, n in sibs:
        arrived(piece(yo, 1 - c, k), sib_s.at[n], sib_r.at[n])
    own.wait()

    acc[...] = jnp.zeros_like(acc)

    def multiply(i, carry):
        step, xe = i // NX, i % NX
        pe = step * first % NH
        s = slot(xe, pe)

        @pl.when(xe != 0)
        def _():
            arrived(zpart(s), wz_s.at[0], wz_r.at[s])

        @pl.when(pe != 0)
        def _():
            arrived(xpart(s), wx_s.at[0], wx_r.at[s])

        cols = pl.ds(pl.multiple_of(s * CHUNK, 128), CHUNK)
        acc[...] += jnp.dot(rall[:, cols], w[s], preferred_element_type=jnp.float32)
        return carry

    lax.fori_loop(0, SLOTS, multiply, 0)

    part = acc[ROWS:]
    amax = jnp.max(jnp.max(jnp.abs(part), axis=0, keepdims=True), axis=1, keepdims=True)
    unit = jnp.maximum(amax, 1e-30) / 32760.0
    pout[...] = jnp.floor(part * (1.0 / unit) + 0.5).astype(jnp.int32).astype(jnp.int16)
    kout[...] = jnp.broadcast_to(unit, kout.shape)
    send(pout, pin, p_s, p_r, mate)
    send(kout, kin, k_s, k_r, mate)
    arrived(pin, p_s, p_r)
    arrived(kin, k_s, k_r)
    projected = acc[:ROWS] + pin[...].astype(jnp.int32).astype(jnp.float32) * kin[0:1, 0:1]
    out[...] = projected.astype(out.dtype)

    def over_columns(v):
        return jnp.sum((v[:, :128] + v[:, 128:]).T, axis=0, keepdims=True)

    s0[0:1] = over_columns(projected * projected)
    s0[1:2] = over_columns(projected * head[...].astype(jnp.float32).reshape(1, COLS))
    send(s0, s1, sc_s.at[0], sc_r.at[0], sibling)
    arrived(s1, sc_s.at[0], sc_r.at[0])
    here = zh * NY + y
    ys[here] = s0[...] + s1[...]
    for n, (e, g) in enumerate(group, 1):
        send(ys.at[here], ys.at[here], sc_s.at[n], sc_r.at[n], at_group(e, g))
    for n, (e, g) in enumerate(group, 1):
        arrived(ys.at[(zh + g) % 2 * NY + (y - e + NY) % NY], sc_s.at[n], sc_r.at[n])
    total = jnp.sum(ys[...], axis=0)
    scores[...] = total[1:2] / jnp.sqrt(total[0:1] / D + 1e-06)

    for copy in sent:
        copy.wait_send()


def results(out_in, scores_in, out, scores):
    out[...] = out_in[...]
    scores[...] = scores_in[...]


def on_device(codes, offsets, responses, head):
    vmem = pl.BlockSpec(memory_space=pltpu.VMEM)
    dma = pltpu.SemaphoreType.DMA
    f32, bf16 = jnp.float32, jnp.bfloat16
    out, scores = pl.pallas_call(
        kernel,
        out_shape=(
            jax.ShapeDtypeStruct((ROWS, COLS), bf16),
            jax.ShapeDtypeStruct((1, ROWS), f32),
        ),
        in_specs=[vmem, vmem, pl.BlockSpec(memory_space=pl.ANY), vmem],
        out_specs=(vmem, vmem),
        scratch_shapes=[
            pltpu.VMEM((2 * ROWS, HALF), bf16),
            pltpu.VMEM((SLOTS, CHUNK, COLS), bf16),
            pltpu.VMEM((2 * ROWS, COLS), f32),
            pltpu.VMEM((ROWS, COLS), jnp.int16),
            pltpu.VMEM((ROWS, COLS), jnp.int16),
            pltpu.VMEM((8, 128), f32),
            pltpu.VMEM((8, 128), f32),
            pltpu.VMEM((2, ROWS), f32),
            pltpu.VMEM((2, ROWS), f32),
            pltpu.VMEM((2 * NY, 2, ROWS), f32),
            dma,
            dma((2,)), dma((2,)),
            dma((16,)), dma((16,)),
            dma((16,)), dma((16,)),
            dma((12,)), dma((SLOTS,)),
            dma((12,)), dma((SLOTS,)),
            dma, dma,
            dma, dma,
            dma((2 * NY,)), dma((2 * NY,)),
        ],
        compiler_params=pltpu.CompilerParams(
            collective_id=0, has_side_effects=True, vmem_limit_bytes=60 * 2**20
        ),
        cost_estimate=pl.CostEstimate(flops=2 * ROWS * 2 * HALF * COLS, bytes_accessed=8 * 2**20, transcendentals=0),
        name="project_and_score",
    )(codes, offsets.T, responses, head)
    out, scores = pl.pallas_call(
        results,
        out_shape=(
            jax.ShapeDtypeStruct((ROWS, COLS), bf16),
            jax.ShapeDtypeStruct((1, ROWS), f32),
        ),
        name="results",
    )(out, scores)
    return out, scores.reshape(ROWS)


def solution(mesh):
    in_specs = (P("fsdp", "tp"), P("fsdp", "tp"), P("fsdp", None), P("tp"))
    out_specs = (P("fsdp", "tp"), P("fsdp"))
    return jax.shard_map(
        on_device, mesh=mesh, in_specs=in_specs, out_specs=out_specs, check_vma=False
    )
```

```python
import jax
import jax.numpy as jnp
from jax import lax
from jax.experimental import pallas as pl
from jax.experimental.pallas import tpu as pltpu
from jax.sharding import PartitionSpec as P

MESH = pl.DeviceIdType.MESH
BLK = 128
D = 8192
NX, NY, NZ, NH = 4, 8, 6, 3
ROWS = 256
CHUNK = 640
COLS = 256
HALF = NX * NH * CHUNK
SLOTS = NX * NH
ZF = 464
PARTS = ((0, ZF), (0, 240), (240, ZF - 240), (ZF, CHUNK - ZF), (ZF, 96), (ZF + 96, CHUNK - ZF - 96))
ZALL, ZTOP, ZLOW, XALL, XTOP, XLOW = range(len(PARTS))
SUBS = 4
SUB = HALF // SUBS
PIECE = ROWS // (2 * NY)


def device(x, y, zl, zh, c):
    return (zl * NX + x, (zh * NY + y) * 2 + c)


def kernel(
    codes, offsets, responses, head, out, scores,
    rall, w, acc, pout, pin, kout, kin, ys, zs,
    own_sem, inj_s, inj_r, ring_s, ring_r, sib_s, sib_r,
    w_s, w_r, p_s, p_r, k_s, k_r, sc_s, sc_r,
):
    f, t = lax.axis_index("fsdp"), lax.axis_index("tp")
    x, zl = f % NX, f // NX
    c, y, zh = t % 2, (t // 2) % NY, t // (2 * NY)
    h, p = zl // NH, zl % NH

    sibling = device(x, y, zl, zh, 1 - c)

    def at_x(e):
        return device((x + e) % NX, y, zl, zh, c)

    def at_z(e):
        return device(x, y, h * NH + (p + e) % NH, zh, c)

    def at_y(e):
        return device(x, (y + e + NY) % NY, zl, zh, c)

    mate = device(x, y, NZ - 1 - zl, zh, c)
    outer, middle = (zl == 0) | (zl == NZ - 1), (zl == NH - 1) | (zl == NH)
    wants = [
        device(x, y, NZ - 1 - zl, jnp.where(outer, 1 - zh, zh), c),
        device(x, y, NZ - 1 - zl, jnp.where(middle, zh, 1 - zh), c),
    ]
    rest = [device(x, y, zl, (zh + g) % 2, (c + k) % 2) for g, k in ((0, 1), (1, 0), (1, 1))]

    barrier = pltpu.get_barrier_semaphore()
    partners = [mate, *wants, *rest, at_x(1), at_x(3)]
    partners += [at_z(e) for e in range(1, NH)]
    partners += [at_y(e) for e in range(1, NY)]
    for partner in partners:
        pl.semaphore_signal(barrier, inc=1, device_id=partner, device_id_type=MESH)

    own = pltpu.make_async_copy(
        responses.at[:, pl.ds(pl.multiple_of(h * HALF, 128), HALF)],
        rall.at[pl.ds(0, ROWS)],
        own_sem,
    )
    own.start()

    def slot(xe, pe):
        return ((p + pe) % NH) * NX + (x + xe) % NX

    mine = slot(0, 0)
    for i in range(CHUNK // BLK):
        for j in range(COLS // BLK):
            block = codes[i * BLK : (i + 1) * BLK, j * BLK : (j + 1) * BLK].astype(jnp.float32)
            amax = jnp.max(jnp.max(jnp.abs(block), axis=0, keepdims=True), axis=1, keepdims=True)
            scale = jnp.exp2(offsets[j : j + 1, i : i + 1].astype(jnp.float32)) / (amax + 1e-06)
            w[mine, i * BLK : (i + 1) * BLK, j * BLK : (j + 1) * BLK] = (block * scale).astype(jnp.bfloat16)

    pl.semaphore_wait(barrier, len(partners))

    sent = []

    def send(src, dst, send_sem, recv_sem, to):
        copy = pltpu.make_async_remote_copy(
            src_ref=src, dst_ref=dst, send_sem=send_sem, recv_sem=recv_sem,
            device_id=to, device_id_type=MESH,
        )
        copy.start()
        sent.append(copy)

    def arrived(dst, send_sem, recv_sem):
        pltpu.make_async_remote_copy(
            src_ref=dst, dst_ref=dst, send_sem=send_sem, recv_sem=recv_sem,
            device_id=sibling, device_id_type=MESH,
        ).wait_recv()

    def piece(yo, core, k):
        row = pl.multiple_of(ROWS + 2 * PIECE * yo + PIECE * core, PIECE)
        return rall.at[pl.ds(row, PIECE), pl.ds(k * SUB, SUB)]

    def part(kind, s):
        row, rows = PARTS[kind]
        return w.at[s, pl.ds(row, rows)]

    count = {"w": 0, "ring": 0}

    def send_w(kind, s, to):
        n = count["w"]
        count["w"] += 1
        send(part(kind, s), part(kind, s), w_s.at[n], w_r.at[kind, s], to)

    def arrived_w(kind, s):
        arrived(part(kind, s), w_s.at[0], w_r.at[kind, s])

    def send_rows(k):
        row = pl.multiple_of(2 * PIECE * y + PIECE * c, PIECE)
        col = pl.multiple_of((1 - h) * HALF + k * SUB, 128)
        send(
            responses.at[pl.ds(row, PIECE), pl.ds(col, SUB)],
            piece(y, c, k), inj_s.at[k], inj_r.at[k], wants[k % 2],
        )

    near = jnp.where(p == NH - 1, 2, 1)
    far = NH - near

    send_rows(0)
    send_rows(1)
    for e in (1, 3):
        send_w(XALL, mine, at_x(e))
    for e in (near, far):
        send_w(ZALL, mine, at_z(e))
    for e in (1, 3):
        send_w(ZALL, mine, at_x(e))
    send_rows(2)
    send_rows(3)
    for e in (near, far):
        send_w(XALL, mine, at_z(e))

    sibs = []

    def steps(dir_, k):
        return 4 if (dir_ == 1) == (k % 2 == 0) else 3

    def ring(dir_, k, d):
        yo = (y - dir_ * d + NY) % NY
        ref = piece(yo, c, k)
        i = ((0 if dir_ == 1 else 1) * SUBS + k) * 4
        if d > 0:
            arrived(ref, ring_s.at[i + d - 1], ring_r.at[i + d - 1])
        if d < steps(dir_, k):
            send(ref, ref, ring_s.at[i + d], ring_r.at[i + d], at_y(dir_))
        if d > 0 or dir_ == 1:
            n = count["ring"]
            count["ring"] += 1
            send(ref, ref, sib_s.at[n], sib_r.at[n], sibling)
            sibs.append((yo, k, n))

    def ring_start(*ks):
        for k in ks:
            arrived(piece(y, c, k), inj_s.at[k], inj_r.at[k])
            ring(1, k, 0)
            ring(-1, k, 0)

    def ring_step(d, *ks):
        for k in ks:
            for dir_ in (1, -1):
                if d <= steps(dir_, k):
                    ring(dir_, k, d)

    def pass_x(whole, top, low, pe):
        for xe, half, to in ((1, low, 3), (3, top, 1)):
            arrived_w(whole, slot(xe, pe))
            send_w(half, slot(xe, pe), at_x(to))

    def turn_z(xe):
        for e in (near, far):
            send_w(XALL, slot(xe, 0), at_z(e))

    def turn_x(pe):
        arrived_w(ZALL, slot(0, pe))
        for e in (1, 3):
            send_w(ZALL, slot(0, pe), at_x(e))

    pass_x(XALL, XTOP, XLOW, 0)
    turn_z(1)
    turn_z(3)
    ring_start(0, 1)
    ring_step(1, 0, 1)
    turn_x(near)
    ring_start(2, 3)
    ring_step(2, 0, 1)
    pass_x(ZALL, ZTOP, ZLOW, 0)
    ring_step(1, 2, 3)
    arrived_w(XTOP, slot(2, 0))
    arrived_w(XLOW, slot(2, 0))
    turn_z(2)
    ring_step(3, 0, 1)
    turn_x(far)
    ring_step(2, 2, 3)
    pass_x(ZALL, ZTOP, ZLOW, near)
    ring_step(4, 0, 1)
    ring_step(3, 2, 3)
    pass_x(ZALL, ZTOP, ZLOW, far)
    ring_step(4, 2, 3)
    for yo, k, n in sibs:
        arrived(piece(yo, 1 - c, k), sib_s.at[n], sib_r.at[n])
    own.wait()

    acc[...] = jnp.zeros_like(acc)

    def multiply(i, carry):
        step, xe = i // NX, i % NX
        xe = jnp.where(xe < 2, xe, 5 - xe)
        s = slot(xe, step * near % NH)

        @pl.when(xe == 2)
        def _():
            arrived_w(ZTOP, s)
            arrived_w(ZLOW, s)

        @pl.when(step != 0)
        def _():
            arrived_w(XALL, s)

        cols = pl.ds(pl.multiple_of(s * CHUNK, 128), CHUNK)
        acc[...] += jnp.dot(rall[:, cols], w[s], preferred_element_type=jnp.float32)
        return carry

    lax.fori_loop(0, SLOTS, multiply, 0)

    sums = acc[ROWS:]
    amax = jnp.max(jnp.max(jnp.abs(sums), axis=0, keepdims=True), axis=1, keepdims=True)
    unit = jnp.maximum(amax, 1e-30) / 32760.0
    pout[...] = jnp.floor(sums * (1.0 / unit) + 0.5).astype(jnp.int32).astype(jnp.int16)
    kout[...] = jnp.broadcast_to(unit, kout.shape)
    send(pout, pin, p_s, p_r, mate)
    send(kout, kin, k_s, k_r, mate)
    arrived(pin, p_s, p_r)
    arrived(kin, k_s, k_r)
    projected = acc[:ROWS] + pin[...].astype(jnp.int32).astype(jnp.float32) * kin[0:1, 0:1]
    out[...] = projected.astype(out.dtype)

    def over_columns(v):
        return jnp.sum((v[:, :128] + v[:, 128:]).T, axis=0, keepdims=True)

    ys[y, 0:1] = over_columns(projected * projected)
    ys[y, 1:2] = over_columns(projected * head[...].astype(jnp.float32).reshape(1, COLS))
    for e in range(1, NY):
        send(ys.at[y], ys.at[y], sc_s.at[e], sc_r.at[e], at_y(e))
    for e in range(1, NY):
        arrived(ys.at[(y - e + NY) % NY], sc_s.at[e], sc_r.at[e])
    here = zh * 2 + c
    zs[here] = jnp.sum(ys[...], axis=0)
    for n, to in enumerate(rest):
        send(zs.at[here], zs.at[here], sc_s.at[NY + n], sc_r.at[NY + n], to)
    for n, (g, k) in enumerate(((0, 1), (1, 0), (1, 1))):
        arrived(zs.at[(zh + g) % 2 * 2 + (c + k) % 2], sc_s.at[NY + n], sc_r.at[NY + n])
    total = jnp.sum(zs[...], axis=0)
    scores[...] = total[1:2] / jnp.sqrt(total[0:1] / D + 1e-06)

    for copy in sent:
        copy.wait_send()


def results(out_in, scores_in, out, scores):
    out[...] = out_in[...]
    scores[...] = scores_in[...]


def on_device(codes, offsets, responses, head):
    vmem = pl.BlockSpec(memory_space=pltpu.VMEM)
    dma = pltpu.SemaphoreType.DMA
    f32, bf16 = jnp.float32, jnp.bfloat16
    out, scores = pl.pallas_call(
        kernel,
        out_shape=(
            jax.ShapeDtypeStruct((ROWS, COLS), bf16),
            jax.ShapeDtypeStruct((1, ROWS), f32),
        ),
        in_specs=[vmem, vmem, pl.BlockSpec(memory_space=pl.ANY), vmem],
        out_specs=(vmem, vmem),
        scratch_shapes=[
            pltpu.VMEM((2 * ROWS, HALF), bf16),
            pltpu.VMEM((SLOTS, CHUNK, COLS), bf16),
            pltpu.VMEM((2 * ROWS, COLS), f32),
            pltpu.VMEM((ROWS, COLS), jnp.int16),
            pltpu.VMEM((ROWS, COLS), jnp.int16),
            pltpu.VMEM((8, 128), f32),
            pltpu.VMEM((8, 128), f32),
            pltpu.VMEM((NY, 2, ROWS), f32),
            pltpu.VMEM((4, 2, ROWS), f32),
            dma,
            dma((SUBS,)), dma((SUBS,)),
            dma((8 * SUBS,)), dma((8 * SUBS,)),
            dma((8 * SUBS,)), dma((8 * SUBS,)),
            dma((2 * SLOTS + 4,)), dma((len(PARTS), SLOTS)),
            dma, dma,
            dma, dma,
            dma((NY + 3,)), dma((NY + 3,)),
        ],
        compiler_params=pltpu.CompilerParams(
            collective_id=0, has_side_effects=True, vmem_limit_bytes=60 * 2**20
        ),
        cost_estimate=pl.CostEstimate(flops=2 * ROWS * 2 * HALF * COLS, bytes_accessed=8 * 2**20, transcendentals=0),
        name="project_and_score",
    )(codes, offsets.T, responses, head)
    out, scores = pl.pallas_call(
        results,
        out_shape=(
            jax.ShapeDtypeStruct((ROWS, COLS), bf16),
            jax.ShapeDtypeStruct((1, ROWS), f32),
        ),
        name="results",
    )(out, scores)
    return out, scores.reshape(ROWS)


def solution(mesh):
    in_specs = (P("fsdp", "tp"), P("fsdp", "tp"), P("fsdp", None), P("tp"))
    out_specs = (P("fsdp", "tp"), P("fsdp"))
    return jax.shard_map(
        on_device, mesh=mesh, in_specs=in_specs, out_specs=out_specs, check_vma=False
    )
```

```python
import jax
import jax.numpy as jnp
from jax import lax
from jax.experimental import pallas as pl
from jax.experimental.pallas import tpu as pltpu
from jax.sharding import PartitionSpec as P

MESH = pl.DeviceIdType.MESH
BLK = 128
D = 8192
NX, NY, NZ, NH = 4, 8, 6, 3
ROWS = 256
CHUNK = 640
COLS = 256
HALF = NX * NH * CHUNK
SLOTS = NX * NH
ZF = 496
ZT, XT = (ZF // 2 + 15) // 16 * 16, ((CHUNK - ZF) // 2 + 15) // 16 * 16
PARTS = ((0, ZF), (0, ZT), (ZT, ZF - ZT), (ZF, CHUNK - ZF), (ZF, XT), (ZF + XT, CHUNK - ZF - XT))
ZALL, ZTOP, ZLOW, XALL, XTOP, XLOW = range(len(PARTS))
SUBS = 4
SUB = HALF // SUBS
PIECE = ROWS // (2 * NY)
PLANE = NX * CHUNK
ORDER = (
    ("rows", 0), ("x", XALL, 1), ("x", ZALL, 1), ("rows", 1),
    ("z", ZALL, "near"), ("x", ZALL, 3), ("rows", 2), ("rows", 3),
    ("z", ZALL, "far"), ("start", 0), ("x", XALL, 3), ("start", 1),
    ("pass", ZALL, "own", 3), ("pass", ZALL, "own", 1), ("ring", -1, 1, 1), ("ring", 1, 0, 1),
    ("ring", 1, 1, 1), ("ring", -1, 0, 1), ("pass", XALL, "own", 3), ("start", 2),
    ("turn_x", "near"), ("ring", -1, 0, 2), ("ring", 1, 0, 2), ("turn_z", 3),
    ("turn_z", 0), ("turn_z", 1), ("ring", 1, 2, 1), ("start", 3),
    ("ring", -1, 1, 2), ("ring", 1, 2, 2), ("pass", XALL, "own", 1), ("ring", -1, 3, 1),
    ("ring", 1, 0, 3), ("ring", -1, 2, 1), ("ring", 1, 1, 2), ("turn_x", "far"),
    ("ring", 1, 3, 1), ("pass", ZALL, "near", 3), ("ring", 1, 2, 3), ("ring", -1, 3, 2),
    ("ring", -1, 1, 3), ("ring", 1, 0, 4), ("ring", -1, 3, 3), ("ring", -1, 2, 2),
    ("ring", 1, 3, 2), ("ring", -1, 1, 4), ("pass", ZALL, "near", 1), ("turn_z", 2),
    ("product",), ("ring", 1, 2, 4), ("ring", -1, 0, 3), ("pass", ZALL, "far", 3),
    ("pass", ZALL, "far", 1), ("ring", 1, 3, 3), ("ring", -1, 3, 4), ("ring", -1, 2, 3),
    ("ring", 1, 1, 3),
)


def device(x, y, zl, zh, c):
    return (zl * NX + x, (zh * NY + y) * 2 + c)


def kernel(
    codes_in, offsets_in, responses, head_in, out, scores,
    codes, offsets, head, projected_out, in_sem, out_sem,
    rall, w, acc, pout, pin, kout, kin, ys, zs,
    own_sem, inj_s, inj_r, ring_s, ring_r, sib_s, sib_r,
    w_s, w_r, p_s, p_r, k_s, k_r, sc_s, sc_r,
):
    f, t = lax.axis_index("fsdp"), lax.axis_index("tp")
    x, zl = f % NX, f // NX
    c, y, zh = t % 2, (t // 2) % NY, t // (2 * NY)
    h, p = zl // NH, zl % NH

    sibling = device(x, y, zl, zh, 1 - c)

    def at_x(e):
        return device((x + e) % NX, y, zl, zh, c)

    def at_z(e):
        return device(x, y, h * NH + (p + e) % NH, zh, c)

    def at_y(e):
        return device(x, (y + e + NY) % NY, zl, zh, c)

    mate = device(x, y, NZ - 1 - zl, zh, c)
    outer, middle = (zl == 0) | (zl == NZ - 1), (zl == NH - 1) | (zl == NH)
    wants = [
        device(x, y, NZ - 1 - zl, jnp.where(outer, 1 - zh, zh), c),
        device(x, y, NZ - 1 - zl, jnp.where(middle, zh, 1 - zh), c),
    ]
    rest = [device(x, y, zl, (zh + g) % 2, (c + k) % 2) for g, k in ((0, 1), (1, 0), (1, 1))]

    barrier = pltpu.get_barrier_semaphore()
    partners = [mate, *wants, *rest, at_x(1), at_x(3)]
    partners += [at_z(e) for e in range(1, NH)]
    partners += [at_y(e) for e in range(1, NY)]
    for partner in partners:
        pl.semaphore_signal(barrier, inc=1, device_id=partner, device_id_type=MESH)

    inputs = [
        pltpu.make_async_copy(src, dst, in_sem.at[n])
        for n, (src, dst) in enumerate(((codes_in, codes), (offsets_in, offsets), (head_in, head)))
    ]
    for copy in inputs:
        copy.start()
    own = pltpu.make_async_copy(
        responses.at[:, pl.ds(pl.multiple_of(h * HALF, 128), HALF)],
        rall.at[pl.ds(0, ROWS)],
        own_sem,
    )
    own.start()

    def slot(xe, pe):
        return ((p + pe) % NH) * NX + (x + xe) % NX

    mine = slot(0, 0)
    for copy in inputs:
        copy.wait()
    for i in range(CHUNK // BLK):
        for j in range(COLS // BLK):
            block = codes[i * BLK : (i + 1) * BLK, j * BLK : (j + 1) * BLK].astype(jnp.float32)
            amax = jnp.max(jnp.max(jnp.abs(block), axis=0, keepdims=True), axis=1, keepdims=True)
            scale = jnp.exp2(offsets[j : j + 1, i : i + 1].astype(jnp.float32)) / (amax + 1e-06)
            w[mine, i * BLK : (i + 1) * BLK, j * BLK : (j + 1) * BLK] = (block * scale).astype(jnp.bfloat16)

    pl.semaphore_wait(barrier, len(partners))

    sent = []

    def send(src, dst, send_sem, recv_sem, to):
        copy = pltpu.make_async_remote_copy(
            src_ref=src, dst_ref=dst, send_sem=send_sem, recv_sem=recv_sem,
            device_id=to, device_id_type=MESH,
        )
        copy.start()
        sent.append(copy)

    def arrived(dst, send_sem, recv_sem):
        pltpu.make_async_remote_copy(
            src_ref=dst, dst_ref=dst, send_sem=send_sem, recv_sem=recv_sem,
            device_id=sibling, device_id_type=MESH,
        ).wait_recv()

    def piece(yo, core, k):
        row = pl.multiple_of(ROWS + 2 * PIECE * yo + PIECE * core, PIECE)
        return rall.at[pl.ds(row, PIECE), pl.ds(k * SUB, SUB)]

    def part(kind, s):
        row, rows = PARTS[kind]
        return w.at[s, pl.ds(row, rows)]

    count = {"w": 0, "ring": 0}

    def send_w(kind, s, to):
        n = count["w"]
        count["w"] += 1
        send(part(kind, s), part(kind, s), w_s.at[n], w_r.at[kind, s], to)

    met = set()

    def arrived_w(kind, xe, plane):
        if (kind, xe, plane) not in met:
            met.add((kind, xe, plane))
            s = slot(xe, planes[plane])
            arrived(part(kind, s), w_s.at[0], w_r.at[kind, s])

    def send_rows(k):
        row = pl.multiple_of(2 * PIECE * y + PIECE * c, PIECE)
        col = pl.multiple_of((1 - h) * HALF + k * SUB, 128)
        send(
            responses.at[pl.ds(row, PIECE), pl.ds(col, SUB)],
            piece(y, c, k), inj_s.at[k], inj_r.at[k], wants[k % 2],
        )

    near = jnp.where(p == NH - 1, 2, 1)
    far = NH - near

    planes = {"own": 0, "near": near, "far": far}
    sibs = []

    def steps(dir_, k):
        return 4 if (dir_ == 1) == (k % 2 == 0) else 3

    def ring(dir_, k, d):
        yo = (y - dir_ * d + NY) % NY
        ref = piece(yo, c, k)
        i = ((0 if dir_ == 1 else 1) * SUBS + k) * 4
        if d > 0:
            arrived(ref, ring_s.at[i + d - 1], ring_r.at[i + d - 1])
        if d < steps(dir_, k):
            send(ref, ref, ring_s.at[i + d], ring_r.at[i + d], at_y(dir_))
        if d > 0 or dir_ == 1:
            n = count["ring"]
            count["ring"] += 1
            send(ref, ref, sib_s.at[n], sib_r.at[n], sibling)
            sibs.append((yo, k, n))

    def ring_start(k):
        arrived(piece(y, c, k), inj_s.at[k], inj_r.at[k])
        ring(1, k, 0)
        ring(-1, k, 0)

    def start_x(kind, to):
        send_w(kind, mine, at_x(to))

    def start_z(kind, plane):
        send_w(kind, mine, at_z(planes[plane]))

    def pass_x(kind, plane, xe):
        arrived_w(kind, xe, plane)
        half = {(XALL, 1): XLOW, (XALL, 3): XTOP, (ZALL, 1): ZLOW, (ZALL, 3): ZTOP}[kind, xe]
        send_w(half, slot(xe, planes[plane]), at_x(NX - xe))

    def turn_z(xe):
        if xe:
            for kind in (XTOP, XLOW) if xe == 2 else (XALL,):
                arrived_w(kind, xe, "own")
        for plane in ("near", "far"):
            send_w(XALL, slot(xe, 0), at_z(planes[plane]))

    def turn_x(plane):
        arrived_w(ZALL, 0, plane)
        for to in (1, 3):
            send_w(ZALL, slot(0, planes[plane]), at_x(to))

    def whole_plane(plane):
        for xe in range(NX):
            if xe or plane != "own":
                for kind in (ZTOP, ZLOW) if xe == 2 else (ZALL,):
                    arrived_w(kind, xe, plane)
                for kind in (XTOP, XLOW) if xe == 2 and plane == "own" else (XALL,):
                    arrived_w(kind, xe, plane)
        return (p + planes[plane]) % NH

    def product(first, rows, q):
        cols = pl.ds(pl.multiple_of(q * PLANE, 128), PLANE)
        weights = w[pl.ds(q * NX, NX)].reshape(PLANE, COLS)
        return jnp.dot(rall[pl.ds(first, rows), cols], weights, preferred_element_type=jnp.float32)

    def own_rows():
        own.wait()
        acc[:ROWS] = product(0, ROWS, whole_plane("own"))

    steps_of = {
        "rows": send_rows, "start": ring_start, "ring": ring, "x": start_x, "z": start_z,
        "pass": pass_x, "turn_z": turn_z, "turn_x": turn_x, "product": own_rows,
    }
    for name, *what in ORDER:
        steps_of[name](*what)

    for yo, k, n in sibs:
        arrived(piece(yo, 1 - c, k), sib_s.at[n], sib_r.at[n])
    acc[ROWS:] = product(ROWS, ROWS, (p + 0) % NH)
    for plane in ("near", "far"):
        acc[...] += product(0, 2 * ROWS, whole_plane(plane))

    sums = acc[ROWS:]
    amax = jnp.max(jnp.max(jnp.abs(sums), axis=0, keepdims=True), axis=1, keepdims=True)
    unit = jnp.maximum(amax, 1e-30) / 32760.0
    pout[...] = jnp.floor(sums * (1.0 / unit) + 0.5).astype(jnp.int32).astype(jnp.int16)
    kout[...] = jnp.broadcast_to(unit, kout.shape)
    send(pout, pin, p_s, p_r, mate)
    send(kout, kin, k_s, k_r, mate)
    arrived(pin, p_s, p_r)
    arrived(kin, k_s, k_r)
    projected = acc[:ROWS] + pin[...].astype(jnp.int32).astype(jnp.float32) * kin[0:1, 0:1]
    projected_out[...] = projected.astype(out.dtype)
    result = pltpu.make_async_copy(projected_out, out, out_sem)
    result.start()

    def over_columns(v):
        return jnp.sum((v[:, :128] + v[:, 128:]).T, axis=0, keepdims=True)

    ys[y, 0:1] = over_columns(projected * projected)
    ys[y, 1:2] = over_columns(projected * head[...].astype(jnp.float32).reshape(1, COLS))
    for e in range(1, NY):
        send(ys.at[y], ys.at[y], sc_s.at[e], sc_r.at[e], at_y(e))
    for e in range(1, NY):
        arrived(ys.at[(y - e + NY) % NY], sc_s.at[e], sc_r.at[e])
    here = zh * 2 + c
    zs[here] = jnp.sum(ys[...], axis=0)
    for n, to in enumerate(rest):
        send(zs.at[here], zs.at[here], sc_s.at[NY + n], sc_r.at[NY + n], to)
    for n, (g, k) in enumerate(((0, 1), (1, 0), (1, 1))):
        arrived(zs.at[(zh + g) % 2 * 2 + (c + k) % 2], sc_s.at[NY + n], sc_r.at[NY + n])
    total = jnp.sum(zs[...], axis=0)
    scores[...] = total[1:2] / jnp.sqrt(total[0:1] / D + 1e-06)

    result.wait()
    for copy in sent:
        copy.wait_send()


def results(out_in, scores_in, out, scores):
    out[...] = out_in[...]
    scores[...] = scores_in[...]


def on_device(codes, offsets, responses, head):
    vmem = pl.BlockSpec(memory_space=pltpu.VMEM)
    hbm = pl.BlockSpec(memory_space=pl.ANY)
    dma = pltpu.SemaphoreType.DMA
    f32, bf16 = jnp.float32, jnp.bfloat16
    out, scores = pl.pallas_call(
        kernel,
        out_shape=(
            jax.ShapeDtypeStruct((ROWS, COLS), bf16),
            jax.ShapeDtypeStruct((1, ROWS), f32),
        ),
        in_specs=[hbm] * 4,
        out_specs=(hbm, vmem),
        scratch_shapes=[
            pltpu.VMEM((CHUNK, COLS), bf16),
            pltpu.VMEM((COLS // BLK, CHUNK // BLK), jnp.int32),
            pltpu.VMEM((COLS,), bf16),
            pltpu.VMEM((ROWS, COLS), bf16),
            dma((3,)), dma,
            pltpu.VMEM((2 * ROWS, HALF), bf16),
            pltpu.VMEM((SLOTS, CHUNK, COLS), bf16),
            pltpu.VMEM((2 * ROWS, COLS), f32),
            pltpu.VMEM((ROWS, COLS), jnp.int16),
            pltpu.VMEM((ROWS, COLS), jnp.int16),
            pltpu.VMEM((8, 128), f32),
            pltpu.VMEM((8, 128), f32),
            pltpu.VMEM((NY, 2, ROWS), f32),
            pltpu.VMEM((4, 2, ROWS), f32),
            dma,
            dma((SUBS,)), dma((SUBS,)),
            dma((8 * SUBS,)), dma((8 * SUBS,)),
            dma((8 * SUBS,)), dma((8 * SUBS,)),
            dma((2 * SLOTS + 4,)), dma((len(PARTS), SLOTS)),
            dma, dma,
            dma, dma,
            dma((NY + 3,)), dma((NY + 3,)),
        ],
        compiler_params=pltpu.CompilerParams(
            collective_id=0, has_side_effects=True, vmem_limit_bytes=60 * 2**20
        ),
        cost_estimate=pl.CostEstimate(flops=2 * ROWS * 2 * HALF * COLS, bytes_accessed=8 * 2**20, transcendentals=0),
        name="project_and_score",
    )(codes, offsets.T, responses, head)
    out, scores = pl.pallas_call(
        results,
        out_shape=(
            jax.ShapeDtypeStruct((ROWS, COLS), bf16),
            jax.ShapeDtypeStruct((1, ROWS), f32),
        ),
        name="results",
    )(out, scores)
    return out, scores.reshape(ROWS)


def solution(mesh):
    in_specs = (P("fsdp", "tp"), P("fsdp", "tp"), P("fsdp", None), P("tp"))
    out_specs = (P("fsdp", "tp"), P("fsdp"))
    return jax.shard_map(
        on_device, mesh=mesh, in_specs=in_specs, out_specs=out_specs, check_vma=False
    )
```

```python
import jax
import jax.numpy as jnp
from jax import lax
from jax.experimental import pallas as pl
from jax.experimental.pallas import tpu as pltpu
from jax.sharding import PartitionSpec as P

MESH = pl.DeviceIdType.MESH
BLK = 128
D = 8192
NX, NY, NZ, NH = 4, 8, 6, 3
ROWS = 256
CHUNK = 640
COLS = 256
HALF = NX * NH * CHUNK
SLOTS = NX * NH
ZF = 464
ZT, XT = (ZF // 2 + 15) // 16 * 16, ((CHUNK - ZF) // 2 + 15) // 16 * 16
PARTS = ((0, ZF), (0, ZT), (ZT, ZF - ZT), (ZF, CHUNK - ZF), (ZF, XT), (ZF + XT, CHUNK - ZF - XT))
ZALL, ZTOP, ZLOW, XALL, XTOP, XLOW = range(len(PARTS))
SUBS = 4
SUB = HALF // SUBS
PIECE = ROWS // (2 * NY)
PLANE = NX * CHUNK
ORDER = (
    ("rows", 0), ("rows", 3), ("rows", 1), ("z", ZALL, "far"),
    ("rows", 2), ("x", XALL, 1), ("x", ZALL, 1), ("x", XALL, 3),
    ("x", ZALL, 3), ("start", 0), ("pass", XALL, "own", 3), ("pass", ZALL, "own", 1),
    ("z", ZALL, "near"), ("start", 1), ("start", 3), ("pass", XALL, "own", 1),
    ("ring", -1, 1, 1), ("ring", 1, 0, 1), ("pass", ZALL, "own", 3), ("turn_z", 1),
    ("ring", -1, 3, 1), ("start", 2), ("word_z",), ("ring", 1, 3, 1),
    ("ring", -1, 1, 2), ("ring", 1, 1, 1), ("turn_x", "near"), ("ring", -1, 0, 1),
    ("ring", 1, 0, 2), ("ring", -1, 3, 2), ("ring", 1, 2, 1), ("product",),
    ("turn_z", 3), ("turn_x", "far"), ("ring", 1, 0, 3), ("ring", -1, 2, 1),
    ("turn_z", 0), ("word_on",), ("ring", 1, 2, 2), ("pass", ZALL, "near", 1),
    ("ring", -1, 1, 3), ("turn_z", 2), ("ring", -1, 2, 2), ("ring", -1, 3, 3),
    ("ring", 1, 3, 2), ("pass", ZALL, "near", 3), ("ring", 1, 1, 2), ("ring", -1, 0, 2),
    ("ring", -1, 1, 4), ("ring", 1, 2, 3), ("ring", 1, 3, 3), ("ring", 1, 1, 3),
    ("ring", 1, 0, 4), ("pass", ZALL, "far", 1), ("pass", ZALL, "far", 3), ("ring", -1, 2, 3),
    ("ring", -1, 0, 3), ("ring", 1, 2, 4), ("ring", -1, 3, 4), ("word_core",),
)


def device(x, y, zl, zh, c):
    return (zl * NX + x, (zh * NY + y) * 2 + c)


def kernel(
    codes_in, offsets_in, responses, head_in, out, scores,
    codes, offsets, head, projected_out, in_sem, out_sem,
    rall, w, acc, pout, pin, kout, kin, ys, zs,
    own_sem, inj_s, inj_r, ring_s, ring_r, sib_s, sib_r,
    w_s, w_r, p_s, p_r, k_s, k_r, sc_s, sc_r, word,
):
    f, t = lax.axis_index("fsdp"), lax.axis_index("tp")
    x, zl = f % NX, f // NX
    c, y, zh = t % 2, (t // 2) % NY, t // (2 * NY)
    h, p = zl // NH, zl % NH

    sibling = device(x, y, zl, zh, 1 - c)

    def at_x(e):
        return device((x + e) % NX, y, zl, zh, c)

    def at_z(e):
        return device(x, y, h * NH + (p + e) % NH, zh, c)

    def at_y(e):
        return device(x, (y + e + NY) % NY, zl, zh, c)

    mate = device(x, y, NZ - 1 - zl, zh, c)
    outer, middle = (zl == 0) | (zl == NZ - 1), (zl == NH - 1) | (zl == NH)
    wants = [
        device(x, y, NZ - 1 - zl, jnp.where(outer, 1 - zh, zh), c),
        device(x, y, NZ - 1 - zl, jnp.where(middle, zh, 1 - zh), c),
    ]
    rest = [device(x, y, zl, (zh + g) % 2, (c + k) % 2) for g, k in ((0, 1), (1, 0), (1, 1))]

    barrier = pltpu.get_barrier_semaphore()
    partners = [sibling, *wants, at_x(1), at_x(3), at_z(1), at_z(2), at_y(1), at_y(-1)]
    for partner in partners:
        pl.semaphore_signal(barrier, inc=1, device_id=partner, device_id_type=MESH)

    inputs = [
        pltpu.make_async_copy(src, dst, in_sem.at[n])
        for n, (src, dst) in enumerate(((codes_in, codes), (offsets_in, offsets), (head_in, head)))
    ]
    for copy in inputs:
        copy.start()
    own = pltpu.make_async_copy(
        responses.at[:, pl.ds(pl.multiple_of(h * HALF, 128), HALF)],
        rall.at[pl.ds(0, ROWS)],
        own_sem,
    )
    own.start()

    def slot(xe, pe):
        return ((p + pe) % NH) * NX + (x + xe) % NX

    mine = slot(0, 0)
    for copy in inputs:
        copy.wait()
    for i in range(CHUNK // BLK):
        for j in range(COLS // BLK):
            block = codes[i * BLK : (i + 1) * BLK, j * BLK : (j + 1) * BLK].astype(jnp.float32)
            amax = jnp.max(jnp.max(jnp.abs(block), axis=0, keepdims=True), axis=1, keepdims=True)
            scale = jnp.exp2(offsets[j : j + 1, i : i + 1].astype(jnp.float32)) / (amax + 1e-06)
            w[mine, i * BLK : (i + 1) * BLK, j * BLK : (j + 1) * BLK] = (block * scale).astype(jnp.bfloat16)

    pl.semaphore_wait(barrier, len(partners))

    def tell(n, *to):
        for one in to:
            pl.semaphore_signal(word.at[n], inc=1, device_id=one, device_id_type=MESH)

    def hear(n, number):
        pl.semaphore_wait(word.at[n], number)

    sent = []

    def send(src, dst, send_sem, recv_sem, to):
        copy = pltpu.make_async_remote_copy(
            src_ref=src, dst_ref=dst, send_sem=send_sem, recv_sem=recv_sem,
            device_id=to, device_id_type=MESH,
        )
        copy.start()
        sent.append(copy)

    def arrived(dst, send_sem, recv_sem):
        pltpu.make_async_remote_copy(
            src_ref=dst, dst_ref=dst, send_sem=send_sem, recv_sem=recv_sem,
            device_id=sibling, device_id_type=MESH,
        ).wait_recv()

    def piece(yo, core, k):
        row = pl.multiple_of(ROWS + 2 * PIECE * yo + PIECE * core, PIECE)
        return rall.at[pl.ds(row, PIECE), pl.ds(k * SUB, SUB)]

    def part(kind, s):
        row, rows = PARTS[kind]
        return w.at[s, pl.ds(row, rows)]

    count = {"w": 0, "ring": 0}

    def send_w(kind, s, to):
        n = count["w"]
        count["w"] += 1
        send(part(kind, s), part(kind, s), w_s.at[n], w_r.at[kind, s], to)

    met = set()

    def arrived_w(kind, xe, plane):
        if (kind, xe, plane) not in met:
            met.add((kind, xe, plane))
            s = slot(xe, planes[plane])
            arrived(part(kind, s), w_s.at[0], w_r.at[kind, s])

    def send_rows(k):
        row = pl.multiple_of(2 * PIECE * y + PIECE * c, PIECE)
        col = pl.multiple_of((1 - h) * HALF + k * SUB, 128)
        send(
            responses.at[pl.ds(row, PIECE), pl.ds(col, SUB)],
            piece(y, c, k), inj_s.at[k], inj_r.at[k], wants[k % 2],
        )

    near = jnp.where(p == NH - 1, 2, 1)
    far = NH - near

    planes = {"own": 0, "near": near, "far": far}
    sibs = []

    def steps(dir_, k):
        return 4 if (dir_ == 1) == (k % 2 == 0) else 3

    def ring(dir_, k, d):
        yo = (y - dir_ * d + NY) % NY
        ref = piece(yo, c, k)
        i = ((0 if dir_ == 1 else 1) * SUBS + k) * 4
        if d > 0:
            arrived(ref, ring_s.at[i + d - 1], ring_r.at[i + d - 1])
        if d < steps(dir_, k):
            send(ref, ref, ring_s.at[i + d], ring_r.at[i + d], at_y(dir_))
        if d > 0 or dir_ == 1:
            n = count["ring"]
            count["ring"] += 1
            send(ref, ref, sib_s.at[n], sib_r.at[n], sibling)
            sibs.append((yo, k, n))

    def ring_start(k):
        arrived(piece(y, c, k), inj_s.at[k], inj_r.at[k])
        ring(1, k, 0)
        ring(-1, k, 0)

    def start_x(kind, to):
        send_w(kind, mine, at_x(to))

    def start_z(kind, plane):
        send_w(kind, mine, at_z(planes[plane]))

    def pass_x(kind, plane, xe):
        arrived_w(kind, xe, plane)
        half = {(XALL, 1): XLOW, (XALL, 3): XTOP, (ZALL, 1): ZLOW, (ZALL, 3): ZTOP}[kind, xe]
        send_w(half, slot(xe, planes[plane]), at_x(NX - xe))

    def turn_z(xe):
        if xe:
            for kind in (XTOP, XLOW) if xe == 2 else (XALL,):
                arrived_w(kind, xe, "own")
        for plane in ("near", "far"):
            send_w(XALL, slot(xe, 0), at_z(planes[plane]))

    def turn_x(plane):
        arrived_w(ZALL, 0, plane)
        for to in (1, 3):
            send_w(ZALL, slot(0, planes[plane]), at_x(to))

    def whole_plane(plane):
        for xe in range(NX):
            if xe or plane != "own":
                for kind in (ZTOP, ZLOW) if xe == 2 else (ZALL,):
                    arrived_w(kind, xe, plane)
                for kind in (XTOP, XLOW) if xe == 2 and plane == "own" else (XALL,):
                    arrived_w(kind, xe, plane)
        return (p + planes[plane]) % NH

    def product(first, rows, q):
        cols = pl.ds(pl.multiple_of(q * PLANE, 128), PLANE)
        weights = w[pl.ds(q * NX, NX)].reshape(PLANE, COLS)
        return jnp.dot(rall[pl.ds(first, rows), cols], weights, preferred_element_type=jnp.float32)

    def own_rows():
        own.wait()
        acc[:ROWS] = product(0, ROWS, whole_plane("own"))

    def word_z():
        tell(0, at_z(1), at_z(2))

    def word_on():
        hear(0, 2)
        tell(1, *wants)

    def word_core():
        hear(1, 2)
        tell(2, sibling)

    steps_of = {
        "rows": send_rows, "start": ring_start, "ring": ring, "x": start_x, "z": start_z,
        "pass": pass_x, "turn_z": turn_z, "turn_x": turn_x, "product": own_rows,
        "word_z": word_z, "word_on": word_on, "word_core": word_core,
    }
    for name, *what in ORDER:
        steps_of[name](*what)

    hear(2, 1)
    for yo, k, n in sibs:
        arrived(piece(yo, 1 - c, k), sib_s.at[n], sib_r.at[n])
    acc[ROWS:] = product(ROWS, ROWS, p)
    for plane in ("near", "far"):
        acc[ROWS:] += product(ROWS, ROWS, whole_plane(plane))

    sums = acc[ROWS:]
    amax = jnp.max(jnp.max(jnp.abs(sums), axis=0, keepdims=True), axis=1, keepdims=True)
    unit = jnp.maximum(amax, 1e-30) / 32760.0
    pout[...] = jnp.floor(sums * (1.0 / unit) + 0.5).astype(jnp.int32).astype(jnp.int16)
    kout[...] = jnp.broadcast_to(unit, kout.shape)
    send(pout, pin, p_s, p_r, mate)
    send(kout, kin, k_s, k_r, mate)
    for plane in ("near", "far"):
        acc[:ROWS] += product(0, ROWS, (p + planes[plane]) % NH)
    arrived(pin, p_s, p_r)
    arrived(kin, k_s, k_r)
    projected = acc[:ROWS] + pin[...].astype(jnp.int32).astype(jnp.float32) * kin[0:1, 0:1]
    projected_out[...] = projected.astype(out.dtype)
    result = pltpu.make_async_copy(projected_out, out, out_sem)
    result.start()

    def over_columns(v):
        return jnp.sum((v[:, :128] + v[:, 128:]).T, axis=0, keepdims=True)

    ys[y, 0:1] = over_columns(projected * projected)
    ys[y, 1:2] = over_columns(projected * head[...].astype(jnp.float32).reshape(1, COLS))
    for e in range(1, NY):
        send(ys.at[y], ys.at[y], sc_s.at[e], sc_r.at[e], at_y(e))
    for e in range(1, NY):
        arrived(ys.at[(y - e + NY) % NY], sc_s.at[e], sc_r.at[e])
    here = zh * 2 + c
    zs[here] = jnp.sum(ys[...], axis=0)
    for n, to in enumerate(rest):
        send(zs.at[here], zs.at[here], sc_s.at[NY + n], sc_r.at[NY + n], to)
    for n, (g, k) in enumerate(((0, 1), (1, 0), (1, 1))):
        arrived(zs.at[(zh + g) % 2 * 2 + (c + k) % 2], sc_s.at[NY + n], sc_r.at[NY + n])
    total = jnp.sum(zs[...], axis=0)
    scores[...] = total[1:2] / jnp.sqrt(total[0:1] / D + 1e-06)

    result.wait()
    for copy in sent:
        copy.wait_send()


def results(out_in, scores_in, out, scores):
    out[...] = out_in[...]
    scores[...] = scores_in[...]


def on_device(codes, offsets, responses, head):
    vmem = pl.BlockSpec(memory_space=pltpu.VMEM)
    hbm = pl.BlockSpec(memory_space=pl.ANY)
    dma = pltpu.SemaphoreType.DMA
    f32, bf16 = jnp.float32, jnp.bfloat16
    out, scores = pl.pallas_call(
        kernel,
        out_shape=(
            jax.ShapeDtypeStruct((ROWS, COLS), bf16),
            jax.ShapeDtypeStruct((1, ROWS), f32),
        ),
        in_specs=[hbm] * 4,
        out_specs=(hbm, vmem),
        scratch_shapes=[
            pltpu.VMEM((CHUNK, COLS), bf16),
            pltpu.VMEM((COLS // BLK, CHUNK // BLK), jnp.int32),
            pltpu.VMEM((COLS,), bf16),
            pltpu.VMEM((ROWS, COLS), bf16),
            dma((3,)), dma,
            pltpu.VMEM((2 * ROWS, HALF), bf16),
            pltpu.VMEM((SLOTS, CHUNK, COLS), bf16),
            pltpu.VMEM((2 * ROWS, COLS), f32),
            pltpu.VMEM((ROWS, COLS), jnp.int16),
            pltpu.VMEM((ROWS, COLS), jnp.int16),
            pltpu.VMEM((8, 128), f32),
            pltpu.VMEM((8, 128), f32),
            pltpu.VMEM((NY, 2, ROWS), f32),
            pltpu.VMEM((4, 2, ROWS), f32),
            dma,
            dma((SUBS,)), dma((SUBS,)),
            dma((8 * SUBS,)), dma((8 * SUBS,)),
            dma((8 * SUBS,)), dma((8 * SUBS,)),
            dma((2 * SLOTS + 4,)), dma((len(PARTS), SLOTS)),
            dma, dma,
            dma, dma,
            dma((NY + 3,)), dma((NY + 3,)),
            pltpu.SemaphoreType.REGULAR((3,)),
        ],
        compiler_params=pltpu.CompilerParams(
            collective_id=0, has_side_effects=True, vmem_limit_bytes=60 * 2**20
        ),
        cost_estimate=pl.CostEstimate(flops=2 * ROWS * 2 * HALF * COLS, bytes_accessed=8 * 2**20, transcendentals=0),
        name="project_and_score",
    )(codes, offsets.T, responses, head)
    out, scores = pl.pallas_call(
        results,
        out_shape=(
            jax.ShapeDtypeStruct((ROWS, COLS), bf16),
            jax.ShapeDtypeStruct((1, ROWS), f32),
        ),
        name="results",
    )(out, scores)
    return out, scores.reshape(ROWS)


def solution(mesh):
    in_specs = (P("fsdp", "tp"), P("fsdp", "tp"), P("fsdp", None), P("tp"))
    out_specs = (P("fsdp", "tp"), P("fsdp"))
    return jax.shard_map(
        on_device, mesh=mesh, in_specs=in_specs, out_specs=out_specs, check_vma=False
    )
```

```python
import jax
import jax.numpy as jnp
from jax import lax
from jax.experimental import pallas as pl
from jax.experimental.pallas import tpu as pltpu
from jax.sharding import PartitionSpec as P

MESH = pl.DeviceIdType.MESH
BLK = 128
D = 8192
NX, NY, NZ, NH = 4, 8, 6, 3
ROWS = 256
CHUNK = 640
COLS = 256
NHALF = 128
HALF = NX * NH * CHUNK
SLOTS = NX * NH
ZF = 480
ZT, XT = (ZF // 2 + 15) // 16 * 16, ((CHUNK - ZF) // 2 + 15) // 16 * 16
PARTS = ((0, ZF), (0, ZT), (ZT, ZF - ZT), (ZF, CHUNK - ZF), (ZF, XT), (ZF + XT, CHUNK - ZF - XT))
ZALL, ZTOP, ZLOW, XALL, XTOP, XLOW = range(len(PARTS))
SUBS = 4
SUB = HALF // SUBS
PIECE = ROWS // (2 * NY)
PLANE = NX * CHUNK
ORDER = (
    ("z", 0, ZALL, "near"), ("z", 0, ZALL, "far"), ("x", 0, XALL, 1), ("rows", 0),
    ("x", 1, XALL, 3), ("rows", 1), ("x", 1, ZALL, 3), ("rows", 3),
    ("x", 1, ZALL, 1), ("turn_x", 0, "near"), ("rows", 2), ("start", 1),
    ("x", 0, XALL, 3), ("start", 0), ("x", 0, ZALL, 1), ("start", 3),
    ("pass", 0, ZALL, "near", 1), ("ring", 1, 0, 1), ("z", 1, ZALL, "far"), ("ring", -1, 0, 1),
    ("z", 1, ZALL, "near"), ("start", 2), ("word_z",), ("pass", 0, XALL, "own", 3),
    ("turn_z", 1, 0), ("turn_z", 0, 3), ("x", 1, XALL, 1), ("pass", 0, XALL, "own", 1),
    ("ring", -1, 1, 1), ("pass", 1, XALL, "own", 1), ("ring", 1, 3, 1), ("turn_z", 1, 1),
    ("pass", 0, ZALL, "near", 3), ("ring", 1, 1, 1), ("ring", -1, 3, 1), ("turn_z", 0, 2),
    ("x", 0, ZALL, 3), ("ring", 1, 2, 1), ("turn_x", 0, "far"), ("ring", 1, 0, 2),
    ("turn_x", 1, "far"), ("ring", -1, 0, 2), ("ring", -1, 3, 2), ("ring", 1, 3, 2),
    ("turn_x", 1, "near"), ("turn_z", 0, 1), ("ring", -1, 1, 2), ("ring", 1, 1, 2),
    ("ring", 1, 2, 2), ("ring", -1, 2, 1), ("pass", 0, ZALL, "own", 1), ("word_on",),
    ("ring", -1, 3, 3), ("pass", 1, XALL, "own", 3), ("ring", -1, 1, 3), ("pass", 0, ZALL, "far", 3),
    ("ring", -1, 0, 3), ("pass", 1, ZALL, "far", 3), ("turn_z", 0, 0), ("ring", 1, 0, 3),
    ("ring", -1, 2, 2), ("ring", 1, 3, 3), ("ring", 1, 2, 3), ("turn_z", 1, 3),
    ("pass", 0, ZALL, "far", 1), ("pass", 0, ZALL, "own", 3), ("turn_z", 1, 2), ("ring", -1, 1, 4),
    ("pass", 1, ZALL, "near", 3), ("ring", 1, 0, 4), ("pass", 1, ZALL, "own", 3), ("ring", 1, 1, 3),
    ("pass", 1, ZALL, "near", 1), ("pass", 1, ZALL, "own", 1), ("pass", 1, ZALL, "far", 1), ("ring", 1, 2, 4),
    ("ring", -1, 2, 3), ("ring", -1, 3, 4), ("word_core",), ("partial", 0),
    ("partial", 1),
)


def device(x, y, zl, zh, c):
    return (zl * NX + x, (zh * NY + y) * 2 + c)


def kernel(
    codes_in, offsets_in, responses, head_in, out, scores,
    codes, offsets, head, projected_out, in_sem, out_sem,
    rall, w, acc, pout, pin, kout, kin, ys, zs,
    own_sem, inj_s, inj_r, ring_s, ring_r, sib_s, sib_r,
    w_s, w_r, p_s, p_r, k_s, k_r, sc_s, sc_r, word,
):
    f, t = lax.axis_index("fsdp"), lax.axis_index("tp")
    x, zl = f % NX, f // NX
    c, y, zh = t % 2, (t // 2) % NY, t // (2 * NY)
    h, p = zl // NH, zl % NH

    sibling = device(x, y, zl, zh, 1 - c)

    def at_x(e):
        return device((x + e) % NX, y, zl, zh, c)

    def at_z(e):
        return device(x, y, h * NH + (p + e) % NH, zh, c)

    def at_y(e):
        return device(x, (y + e + NY) % NY, zl, zh, c)

    mate = device(x, y, NZ - 1 - zl, zh, c)
    outer, middle = (zl == 0) | (zl == NZ - 1), (zl == NH - 1) | (zl == NH)
    wants = [
        device(x, y, NZ - 1 - zl, jnp.where(outer, 1 - zh, zh), c),
        device(x, y, NZ - 1 - zl, jnp.where(middle, zh, 1 - zh), c),
    ]
    rest = [device(x, y, zl, (zh + g) % 2, (c + k) % 2) for g, k in ((0, 1), (1, 0), (1, 1))]

    barrier = pltpu.get_barrier_semaphore()
    partners = [sibling, *wants, at_x(1), at_x(3), at_z(1), at_z(2), at_y(1), at_y(-1)]
    for partner in partners:
        pl.semaphore_signal(barrier, inc=1, device_id=partner, device_id_type=MESH)

    inputs = [
        pltpu.make_async_copy(src, dst, in_sem.at[n])
        for n, (src, dst) in enumerate(((codes_in, codes), (offsets_in, offsets), (head_in, head)))
    ]
    for copy in inputs:
        copy.start()
    own = pltpu.make_async_copy(
        responses.at[:, pl.ds(pl.multiple_of(h * HALF, 128), HALF)],
        rall.at[pl.ds(0, ROWS)],
        own_sem,
    )
    own.start()

    def slot(xe, pe):
        return ((p + pe) % NH) * NX + (x + xe) % NX

    mine = slot(0, 0)
    for copy in inputs:
        copy.wait()
    for i in range(CHUNK // BLK):
        for j in range(COLS // BLK):
            block = codes[i * BLK : (i + 1) * BLK, j * BLK : (j + 1) * BLK].astype(jnp.float32)
            amax = jnp.max(jnp.max(jnp.abs(block), axis=0, keepdims=True), axis=1, keepdims=True)
            scale = jnp.exp2(offsets[j : j + 1, i : i + 1].astype(jnp.float32)) / (amax + 1e-06)
            w[j, mine, i * BLK : (i + 1) * BLK] = (block * scale).astype(jnp.bfloat16)

    pl.semaphore_wait(barrier, len(partners))

    def tell(n, *to):
        for one in to:
            pl.semaphore_signal(word.at[n], inc=1, device_id=one, device_id_type=MESH)

    def hear(n, number):
        pl.semaphore_wait(word.at[n], number)

    sent = []

    def send(src, dst, send_sem, recv_sem, to):
        copy = pltpu.make_async_remote_copy(
            src_ref=src, dst_ref=dst, send_sem=send_sem, recv_sem=recv_sem,
            device_id=to, device_id_type=MESH,
        )
        copy.start()
        sent.append(copy)

    def arrived(dst, send_sem, recv_sem):
        pltpu.make_async_remote_copy(
            src_ref=dst, dst_ref=dst, send_sem=send_sem, recv_sem=recv_sem,
            device_id=sibling, device_id_type=MESH,
        ).wait_recv()

    def piece(yo, core, k):
        row = pl.multiple_of(ROWS + 2 * PIECE * yo + PIECE * core, PIECE)
        return rall.at[pl.ds(row, PIECE), pl.ds(k * SUB, SUB)]

    def part(n, kind, s):
        row, rows = PARTS[kind]
        return w.at[n, s, pl.ds(row, rows)]

    count = {"w": 0, "ring": 0}

    def send_w(n, kind, s, to):
        i = count["w"]
        count["w"] += 1
        send(part(n, kind, s), part(n, kind, s), w_s.at[i], w_r.at[n, kind, s], to)

    met = set()

    def arrived_w(n, kind, xe, plane):
        if (n, kind, xe, plane) not in met:
            met.add((n, kind, xe, plane))
            s = slot(xe, planes[plane])
            arrived(part(n, kind, s), w_s.at[0], w_r.at[n, kind, s])

    def send_rows(k):
        row = pl.multiple_of(2 * PIECE * y + PIECE * c, PIECE)
        col = pl.multiple_of((1 - h) * HALF + k * SUB, 128)
        send(
            responses.at[pl.ds(row, PIECE), pl.ds(col, SUB)],
            piece(y, c, k), inj_s.at[k], inj_r.at[k], wants[k % 2],
        )

    near = jnp.where(p == NH - 1, 2, 1)
    far = NH - near

    planes = {"own": 0, "near": near, "far": far}
    sibs = []

    def steps(dir_, k):
        return 4 if (dir_ == 1) == (k % 2 == 0) else 3

    def ring(dir_, k, d):
        yo = (y - dir_ * d + NY) % NY
        ref = piece(yo, c, k)
        i = ((0 if dir_ == 1 else 1) * SUBS + k) * 4
        if d > 0:
            arrived(ref, ring_s.at[i + d - 1], ring_r.at[i + d - 1])
        if d < steps(dir_, k):
            send(ref, ref, ring_s.at[i + d], ring_r.at[i + d], at_y(dir_))
        if d > 0 or dir_ == 1:
            n = count["ring"]
            count["ring"] += 1
            send(ref, ref, sib_s.at[n], sib_r.at[n], sibling)
            sibs.append((yo, k, n))

    def ring_start(k):
        arrived(piece(y, c, k), inj_s.at[k], inj_r.at[k])
        ring(1, k, 0)
        ring(-1, k, 0)

    def start_x(n, kind, to):
        send_w(n, kind, mine, at_x(to))

    def start_z(n, kind, plane):
        send_w(n, kind, mine, at_z(planes[plane]))

    def pass_x(n, kind, plane, xe):
        arrived_w(n, kind, xe, plane)
        half = {(XALL, 1): XLOW, (XALL, 3): XTOP, (ZALL, 1): ZLOW, (ZALL, 3): ZTOP}[kind, xe]
        send_w(n, half, slot(xe, planes[plane]), at_x(NX - xe))

    def turn_z(n, xe):
        if xe:
            for kind in (XTOP, XLOW) if xe == 2 else (XALL,):
                arrived_w(n, kind, xe, "own")
        for plane in ("near", "far"):
            send_w(n, XALL, slot(xe, 0), at_z(planes[plane]))

    def turn_x(n, plane):
        arrived_w(n, ZALL, 0, plane)
        for to in (1, 3):
            send_w(n, ZALL, slot(0, planes[plane]), at_x(to))

    def whole_plane(n, plane):
        for xe in range(NX):
            if xe or plane != "own":
                for kind in (ZTOP, ZLOW) if xe == 2 else (ZALL,):
                    arrived_w(n, kind, xe, plane)
                for kind in (XTOP, XLOW) if xe == 2 and plane == "own" else (XALL,):
                    arrived_w(n, kind, xe, plane)

    def product(n, first, q):
        cols = pl.ds(pl.multiple_of(q * PLANE, 128), PLANE)
        weights = w[n, pl.ds(q * NX, NX)].reshape(PLANE, NHALF)
        return jnp.dot(rall[pl.ds(first, ROWS), cols], weights, preferred_element_type=jnp.float32)

    def partial(n):
        if n == 0:
            for yo, k, i in sibs:
                arrived(piece(yo, 1 - c, k), sib_s.at[i], sib_r.at[i])
        whole_plane(n, "own")
        sums = product(n, ROWS, p)
        for plane in ("near", "far"):
            whole_plane(n, plane)
            sums += product(n, ROWS, (p + planes[plane]) % NH)
        amax = jnp.max(jnp.max(jnp.abs(sums), axis=0, keepdims=True), axis=1, keepdims=True)
        unit = jnp.maximum(amax, 1e-30) / 32760.0
        pout[n] = jnp.floor(sums * (1.0 / unit) + 0.5).astype(jnp.int32).astype(jnp.int16)
        kout[n] = jnp.broadcast_to(unit, kout.shape[1:])
        send(pout.at[n], pin.at[n], p_s.at[n], p_r.at[n], mate)
        send(kout.at[n], kin.at[n], k_s.at[n], k_r.at[n], mate)

    def word_z():
        tell(0, at_z(1), at_z(2))

    def word_on():
        hear(0, 2)
        tell(1, *wants)

    def word_core():
        hear(1, 2)
        tell(2, sibling)

    steps_of = {
        "rows": send_rows, "start": ring_start, "ring": ring, "x": start_x, "z": start_z,
        "pass": pass_x, "turn_z": turn_z, "turn_x": turn_x, "partial": partial,
        "word_z": word_z, "word_on": word_on, "word_core": word_core,
    }
    for name, *what in ORDER:
        steps_of[name](*what)

    hear(2, 1)
    own.wait()
    acc[...] = jnp.zeros_like(acc)

    def own_rows(i, carry):
        acc[i // NH] += product(i // NH, 0, i % NH)
        return carry

    lax.fori_loop(0, 2 * NH, own_rows, 0)
    halves = []
    for n in range(2):
        arrived(pin.at[n], p_s.at[n], p_r.at[n])
        arrived(kin.at[n], k_s.at[n], k_r.at[n])
        halves.append(acc[n] + pin[n].astype(jnp.int32).astype(jnp.float32) * kin[n, 0:1, 0:1])
        projected_out[:, n * NHALF : (n + 1) * NHALF] = halves[n].astype(out.dtype)
    result = pltpu.make_async_copy(projected_out, out, out_sem)
    result.start()

    def over_columns(v):
        return jnp.sum(v.T, axis=0, keepdims=True)

    heads = head[...].astype(jnp.float32).reshape(1, COLS)
    first, second = halves
    ys[y, 0:1] = over_columns(first * first + second * second)
    ys[y, 1:2] = over_columns(first * heads[:, :NHALF] + second * heads[:, NHALF:])
    for e in range(1, NY):
        send(ys.at[y], ys.at[y], sc_s.at[e], sc_r.at[e], at_y(e))
    for e in range(1, NY):
        arrived(ys.at[(y - e + NY) % NY], sc_s.at[e], sc_r.at[e])
    here = zh * 2 + c
    zs[here] = jnp.sum(ys[...], axis=0)
    for n, to in enumerate(rest):
        send(zs.at[here], zs.at[here], sc_s.at[NY + n], sc_r.at[NY + n], to)
    for n, (g, k) in enumerate(((0, 1), (1, 0), (1, 1))):
        arrived(zs.at[(zh + g) % 2 * 2 + (c + k) % 2], sc_s.at[NY + n], sc_r.at[NY + n])
    total = jnp.sum(zs[...], axis=0)
    scores[...] = total[1:2] / jnp.sqrt(total[0:1] / D + 1e-06)

    result.wait()
    for copy in sent:
        copy.wait_send()


def results(out_in, scores_in, out, scores):
    out[...] = out_in[...]
    scores[...] = scores_in[...]


def on_device(codes, offsets, responses, head):
    vmem = pl.BlockSpec(memory_space=pltpu.VMEM)
    hbm = pl.BlockSpec(memory_space=pl.ANY)
    dma = pltpu.SemaphoreType.DMA
    f32, bf16 = jnp.float32, jnp.bfloat16
    out, scores = pl.pallas_call(
        kernel,
        out_shape=(
            jax.ShapeDtypeStruct((ROWS, COLS), bf16),
            jax.ShapeDtypeStruct((1, ROWS), f32),
        ),
        in_specs=[hbm] * 4,
        out_specs=(hbm, vmem),
        scratch_shapes=[
            pltpu.VMEM((CHUNK, COLS), bf16),
            pltpu.VMEM((COLS // BLK, CHUNK // BLK), jnp.int32),
            pltpu.VMEM((COLS,), bf16),
            pltpu.VMEM((ROWS, COLS), bf16),
            dma((3,)), dma,
            pltpu.VMEM((2 * ROWS, HALF), bf16),
            pltpu.VMEM((2, SLOTS, CHUNK, NHALF), bf16),
            pltpu.VMEM((2, ROWS, NHALF), f32),
            pltpu.VMEM((2, ROWS, NHALF), jnp.int16),
            pltpu.VMEM((2, ROWS, NHALF), jnp.int16),
            pltpu.VMEM((2, 8, 128), f32),
            pltpu.VMEM((2, 8, 128), f32),
            pltpu.VMEM((NY, 2, ROWS), f32),
            pltpu.VMEM((4, 2, ROWS), f32),
            dma,
            dma((SUBS,)), dma((SUBS,)),
            dma((8 * SUBS,)), dma((8 * SUBS,)),
            dma((8 * SUBS,)), dma((8 * SUBS,)),
            dma((4 * SLOTS + 8,)), dma((2, len(PARTS), SLOTS)),
            dma((2,)), dma((2,)),
            dma((2,)), dma((2,)),
            dma((NY + 3,)), dma((NY + 3,)),
            pltpu.SemaphoreType.REGULAR((3,)),
        ],
        compiler_params=pltpu.CompilerParams(
            collective_id=0, has_side_effects=True, vmem_limit_bytes=60 * 2**20
        ),
        cost_estimate=pl.CostEstimate(flops=2 * ROWS * 2 * HALF * COLS, bytes_accessed=8 * 2**20, transcendentals=0),
        name="project_and_score",
    )(codes, offsets.T, responses, head)
    out, scores = pl.pallas_call(
        results,
        out_shape=(
            jax.ShapeDtypeStruct((ROWS, COLS), bf16),
            jax.ShapeDtypeStruct((1, ROWS), f32),
        ),
        name="results",
    )(out, scores)
    return out, scores.reshape(ROWS)


def solution(mesh):
    in_specs = (P("fsdp", "tp"), P("fsdp", "tp"), P("fsdp", None), P("tp"))
    out_specs = (P("fsdp", "tp"), P("fsdp"))
    return jax.shard_map(
        on_device, mesh=mesh, in_specs=in_specs, out_specs=out_specs, check_vma=False
    )
```

```python
import jax
import jax.numpy as jnp
from jax import lax
from jax.experimental import pallas as pl
from jax.experimental.pallas import tpu as pltpu
from jax.sharding import PartitionSpec as P

MESH = pl.DeviceIdType.MESH
BLK = 128
D = 8192
NX, NY, NZ, NH = 4, 8, 6, 3
ROWS = 256
CHUNK = 640
COLS = 256
NHALF = 128
HALF = NX * NH * CHUNK
SLOTS = NX * NH
ZF = 480
ZT, XT = (ZF // 2 + 15) // 16 * 16, ((CHUNK - ZF) // 2 + 15) // 16 * 16
PARTS = ((0, ZF), (0, ZT), (ZT, ZF - ZT), (ZF, CHUNK - ZF), (ZF, XT), (ZF + XT, CHUNK - ZF - XT))
ZALL, ZTOP, ZLOW, XALL, XTOP, XLOW = range(len(PARTS))
SUBS = 4
SUB = HALF // SUBS
PIECE = ROWS // (2 * NY)
PLANE = NX * CHUNK
ORDER = (
    ("z", 0, ZALL, "near"), ("z", 0, ZALL, "far"), ("x", 0, XALL, 1), ("rows", 0),
    ("x", 1, XALL, 3), ("rows", 1), ("x", 1, ZALL, 3), ("rows", 3),
    ("x", 1, ZALL, 1), ("turn_x", 0, "near"), ("rows", 2), ("start", 1),
    ("x", 0, XALL, 3), ("start", 0), ("x", 0, ZALL, 1), ("start", 3),
    ("pass", 0, ZALL, "near", 1), ("ring", 1, 0, 1), ("z", 1, ZALL, "far"), ("ring", -1, 0, 1),
    ("z", 1, ZALL, "near"), ("start", 2), ("word_z",), ("pass", 0, XALL, "own", 3),
    ("turn_z", 1, 0), ("turn_z", 0, 3), ("x", 1, XALL, 1), ("pass", 0, XALL, "own", 1),
    ("ring", -1, 1, 1), ("pass", 1, XALL, "own", 1), ("ring", 1, 3, 1), ("turn_z", 1, 1),
    ("pass", 0, ZALL, "near", 3), ("ring", 1, 1, 1), ("ring", -1, 3, 1), ("turn_z", 0, 2),
    ("x", 0, ZALL, 3), ("ring", 1, 2, 1), ("turn_x", 0, "far"), ("ring", 1, 0, 2),
    ("turn_x", 1, "far"), ("ring", -1, 0, 2), ("ring", -1, 3, 2), ("ring", 1, 3, 2),
    ("turn_x", 1, "near"), ("turn_z", 0, 1), ("ring", -1, 1, 2), ("ring", 1, 1, 2),
    ("ring", 1, 2, 2), ("ring", -1, 2, 1), ("pass", 0, ZALL, "own", 1), ("word_on",),
    ("ring", -1, 3, 3), ("pass", 1, XALL, "own", 3), ("ring", -1, 1, 3), ("pass", 0, ZALL, "far", 3),
    ("ring", -1, 0, 3), ("pass", 1, ZALL, "far", 3), ("turn_z", 0, 0), ("ring", 1, 0, 3),
    ("ring", -1, 2, 2), ("ring", 1, 3, 3), ("ring", 1, 2, 3), ("turn_z", 1, 3),
    ("pass", 0, ZALL, "far", 1), ("pass", 0, ZALL, "own", 3), ("turn_z", 1, 2), ("ring", -1, 1, 4),
    ("pass", 1, ZALL, "near", 3), ("ring", 1, 0, 4), ("pass", 1, ZALL, "own", 3), ("ring", 1, 1, 3),
    ("pass", 1, ZALL, "near", 1), ("pass", 1, ZALL, "own", 1), ("pass", 1, ZALL, "far", 1), ("ring", 1, 2, 4),
    ("ring", -1, 2, 3), ("ring", -1, 3, 4), ("word_core",), ("partial", 0),
    ("partial", 1),
)


def device(x, y, zl, zh, c):
    return (zl * NX + x, (zh * NY + y) * 2 + c)


def kernel(
    codes_in, offsets_in, responses, head_in, out, scores,
    codes, offsets, head, projected_out, in_sem, out_sem,
    rall, w, acc, pout, pin, kout, kin, ys, zs,
    own_sem, inj_s, inj_r, ring_s, ring_r, sib_s, sib_r,
    w_s, w_r, p_s, p_r, k_s, k_r, sc_s, sc_r, word,
):
    f, t = lax.axis_index("fsdp"), lax.axis_index("tp")
    x, zl = f % NX, f // NX
    c, y, zh = t % 2, (t // 2) % NY, t // (2 * NY)
    h, p = zl // NH, zl % NH

    sibling = device(x, y, zl, zh, 1 - c)

    def at_x(e):
        return device((x + e) % NX, y, zl, zh, c)

    def at_z(e):
        return device(x, y, h * NH + (p + e) % NH, zh, c)

    def at_y(e):
        return device(x, (y + e + NY) % NY, zl, zh, c)

    mate = device(x, y, NZ - 1 - zl, zh, c)
    outer, middle = (zl == 0) | (zl == NZ - 1), (zl == NH - 1) | (zl == NH)
    wants = [
        device(x, y, NZ - 1 - zl, jnp.where(outer, 1 - zh, zh), c),
        device(x, y, NZ - 1 - zl, jnp.where(middle, zh, 1 - zh), c),
    ]
    rest = [device(x, y, zl, (zh + g) % 2, (c + k) % 2) for g, k in ((0, 1), (1, 0), (1, 1))]

    barrier = pltpu.get_barrier_semaphore()
    partners = [sibling, *wants, at_x(1), at_x(3), at_z(1), at_z(2), at_y(1), at_y(-1)]
    for partner in partners:
        pl.semaphore_signal(barrier, inc=1, device_id=partner, device_id_type=MESH)

    inputs = [
        pltpu.make_async_copy(src, dst, in_sem.at[n])
        for n, (src, dst) in enumerate(((codes_in, codes), (offsets_in, offsets), (head_in, head)))
    ]
    for copy in inputs:
        copy.start()
    own = pltpu.make_async_copy(
        responses.at[:, pl.ds(pl.multiple_of(h * HALF, 128), HALF)],
        rall.at[pl.ds(0, ROWS)],
        own_sem,
    )
    own.start()

    def slot(xe, pe):
        return ((p + pe) % NH) * NX + (x + xe) % NX

    mine = slot(0, 0)
    for copy in inputs:
        copy.wait()
    for i in range(CHUNK // BLK):
        for j in range(COLS // BLK):
            block = codes[i * BLK : (i + 1) * BLK, j * BLK : (j + 1) * BLK].astype(jnp.float32)
            amax = jnp.max(jnp.max(jnp.abs(block), axis=0, keepdims=True), axis=1, keepdims=True)
            scale = jnp.exp2(offsets[j : j + 1, i : i + 1].astype(jnp.float32)) / (amax + 1e-06)
            w[j, mine, i * BLK : (i + 1) * BLK] = (block * scale).astype(jnp.bfloat16)

    pl.semaphore_wait(barrier, len(partners))

    def tell(n, *to):
        for one in to:
            pl.semaphore_signal(word.at[n], inc=1, device_id=one, device_id_type=MESH)

    def hear(n, number):
        pl.semaphore_wait(word.at[n], number)

    sent = []

    def send(src, dst, send_sem, recv_sem, to):
        copy = pltpu.make_async_remote_copy(
            src_ref=src, dst_ref=dst, send_sem=send_sem, recv_sem=recv_sem,
            device_id=to, device_id_type=MESH,
        )
        copy.start()
        sent.append(copy)

    def arrived(dst, send_sem, recv_sem):
        pltpu.make_async_remote_copy(
            src_ref=dst, dst_ref=dst, send_sem=send_sem, recv_sem=recv_sem,
            device_id=sibling, device_id_type=MESH,
        ).wait_recv()

    def piece(yo, core, k):
        row = pl.multiple_of(ROWS + 2 * PIECE * yo + PIECE * core, PIECE)
        return rall.at[pl.ds(row, PIECE), pl.ds(k * SUB, SUB)]

    def part(n, kind, s):
        row, rows = PARTS[kind]
        return w.at[n, s, pl.ds(row, rows)]

    count = {"w": 0, "ring": 0}

    def send_w(n, kind, s, to):
        i = count["w"]
        count["w"] += 1
        send(part(n, kind, s), part(n, kind, s), w_s.at[i], w_r.at[n, kind, s], to)

    met = set()

    def arrived_w(n, kind, xe, plane):
        if (n, kind, xe, plane) not in met:
            met.add((n, kind, xe, plane))
            s = slot(xe, planes[plane])
            arrived(part(n, kind, s), w_s.at[0], w_r.at[n, kind, s])

    def send_rows(k):
        row = pl.multiple_of(2 * PIECE * y + PIECE * c, PIECE)
        col = pl.multiple_of((1 - h) * HALF + k * SUB, 128)
        send(
            responses.at[pl.ds(row, PIECE), pl.ds(col, SUB)],
            piece(y, c, k), inj_s.at[k], inj_r.at[k], wants[k % 2],
        )

    near = jnp.where(p == NH - 1, 2, 1)
    far = NH - near

    planes = {"own": 0, "near": near, "far": far}
    sibs = []

    def steps(dir_, k):
        return 4 if (dir_ == 1) == (k % 2 == 0) else 3

    def ring(dir_, k, d):
        yo = (y - dir_ * d + NY) % NY
        ref = piece(yo, c, k)
        i = ((0 if dir_ == 1 else 1) * SUBS + k) * 4
        if d > 0:
            arrived(ref, ring_s.at[i + d - 1], ring_r.at[i + d - 1])
        if d < steps(dir_, k):
            send(ref, ref, ring_s.at[i + d], ring_r.at[i + d], at_y(dir_))
        if d > 0 or dir_ == 1:
            n = count["ring"]
            count["ring"] += 1
            send(ref, ref, sib_s.at[n], sib_r.at[n], sibling)
            sibs.append((yo, k, n))

    def ring_start(k):
        arrived(piece(y, c, k), inj_s.at[k], inj_r.at[k])
        ring(1, k, 0)
        ring(-1, k, 0)

    def start_x(n, kind, to):
        send_w(n, kind, mine, at_x(to))

    def start_z(n, kind, plane):
        send_w(n, kind, mine, at_z(planes[plane]))

    def pass_x(n, kind, plane, xe):
        arrived_w(n, kind, xe, plane)
        half = {(XALL, 1): XLOW, (XALL, 3): XTOP, (ZALL, 1): ZLOW, (ZALL, 3): ZTOP}[kind, xe]
        send_w(n, half, slot(xe, planes[plane]), at_x(NX - xe))

    def turn_z(n, xe):
        if xe:
            for kind in (XTOP, XLOW) if xe == 2 else (XALL,):
                arrived_w(n, kind, xe, "own")
        for plane in ("near", "far"):
            send_w(n, XALL, slot(xe, 0), at_z(planes[plane]))

    def turn_x(n, plane):
        arrived_w(n, ZALL, 0, plane)
        for to in (1, 3):
            send_w(n, ZALL, slot(0, planes[plane]), at_x(to))

    def whole_plane(n, plane):
        for xe in range(NX):
            if xe or plane != "own":
                for kind in (ZTOP, ZLOW) if xe == 2 else (ZALL,):
                    arrived_w(n, kind, xe, plane)
                for kind in (XTOP, XLOW) if xe == 2 and plane == "own" else (XALL,):
                    arrived_w(n, kind, xe, plane)

    def product(n, first, q):
        cols = pl.ds(pl.multiple_of(q * PLANE, 128), PLANE)
        weights = w[n, pl.ds(q * NX, NX)].reshape(PLANE, NHALF)
        return jnp.dot(rall[pl.ds(first, ROWS), cols], weights, preferred_element_type=jnp.float32)

    def partial(n):
        if n == 0:
            for yo, k, i in sibs:
                arrived(piece(yo, 1 - c, k), sib_s.at[i], sib_r.at[i])
        whole_plane(n, "own")
        sums = product(n, ROWS, p)
        for plane in ("near", "far"):
            whole_plane(n, plane)
            sums += product(n, ROWS, (p + planes[plane]) % NH)
        amax = jnp.max(jnp.max(jnp.abs(sums), axis=0, keepdims=True), axis=1, keepdims=True)
        unit = jnp.maximum(amax, 1e-30) / 32760.0
        pout[n] = jnp.floor(sums * (1.0 / unit) + 0.5).astype(jnp.int32).astype(jnp.int16)
        kout[n] = jnp.broadcast_to(unit, kout.shape[1:])
        send(pout.at[n], pin.at[n], p_s.at[n], p_r.at[n], mate)
        send(kout.at[n], kin.at[n], k_s.at[n], k_r.at[n], mate)

    def word_z():
        tell(0, at_z(1), at_z(2))

    def word_on():
        hear(0, 2)
        tell(1, *wants)

    def word_core():
        hear(1, 2)
        tell(2, sibling)

    steps_of = {
        "rows": send_rows, "start": ring_start, "ring": ring, "x": start_x, "z": start_z,
        "pass": pass_x, "turn_z": turn_z, "turn_x": turn_x, "partial": partial,
        "word_z": word_z, "word_on": word_on, "word_core": word_core,
    }
    for name, *what in ORDER:
        steps_of[name](*what)

    hear(2, 1)
    own.wait()
    acc[...] = jnp.zeros_like(acc)

    def own_rows(i, carry):
        acc[i // NH] += product(i // NH, 0, i % NH)
        return carry

    lax.fori_loop(0, 2 * NH, own_rows, 0)
    for copy in sent[:-4]:
        copy.wait_send()
    del sent[:-4]
    halves = []
    for n in range(2):
        arrived(pin.at[n], p_s.at[n], p_r.at[n])
        arrived(kin.at[n], k_s.at[n], k_r.at[n])
        halves.append(acc[n] + pin[n].astype(jnp.int32).astype(jnp.float32) * kin[n, 0:1, 0:1])
        projected_out[:, n * NHALF : (n + 1) * NHALF] = halves[n].astype(out.dtype)
    result = pltpu.make_async_copy(projected_out, out, out_sem)
    result.start()

    def over_columns(v):
        return jnp.sum(v.T, axis=0, keepdims=True)

    heads = head[...].astype(jnp.float32).reshape(1, COLS)
    first, second = halves
    ys[y, 0:1] = over_columns(first * first + second * second)
    ys[y, 1:2] = over_columns(first * heads[:, :NHALF] + second * heads[:, NHALF:])
    for e in range(1, NY):
        send(ys.at[y], ys.at[y], sc_s.at[e], sc_r.at[e], at_y(e))
    for e in range(1, NY):
        arrived(ys.at[(y - e + NY) % NY], sc_s.at[e], sc_r.at[e])
    here = zh * 2 + c
    zs[here] = jnp.sum(ys[...], axis=0)
    for n, to in enumerate(rest):
        send(zs.at[here], zs.at[here], sc_s.at[NY + n], sc_r.at[NY + n], to)
    for n, (g, k) in enumerate(((0, 1), (1, 0), (1, 1))):
        arrived(zs.at[(zh + g) % 2 * 2 + (c + k) % 2], sc_s.at[NY + n], sc_r.at[NY + n])
    total = jnp.sum(zs[...], axis=0)
    scores[...] = total[1:2] / jnp.sqrt(total[0:1] / D + 1e-06)

    result.wait()
    for copy in sent:
        copy.wait_send()


def results(out_in, scores_in, out, scores):
    out[...] = out_in[...]
    scores[...] = scores_in[...]


def on_device(codes, offsets, responses, head):
    vmem = pl.BlockSpec(memory_space=pltpu.VMEM)
    hbm = pl.BlockSpec(memory_space=pl.ANY)
    dma = pltpu.SemaphoreType.DMA
    f32, bf16 = jnp.float32, jnp.bfloat16
    out, scores = pl.pallas_call(
        kernel,
        out_shape=(
            jax.ShapeDtypeStruct((ROWS, COLS), bf16),
            jax.ShapeDtypeStruct((1, ROWS), f32),
        ),
        in_specs=[hbm] * 4,
        out_specs=(hbm, vmem),
        scratch_shapes=[
            pltpu.VMEM((CHUNK, COLS), bf16),
            pltpu.VMEM((COLS // BLK, CHUNK // BLK), jnp.int32),
            pltpu.VMEM((COLS,), bf16),
            pltpu.VMEM((ROWS, COLS), bf16),
            dma((3,)), dma,
            pltpu.VMEM((2 * ROWS, HALF), bf16),
            pltpu.VMEM((2, SLOTS, CHUNK, NHALF), bf16),
            pltpu.VMEM((2, ROWS, NHALF), f32),
            pltpu.VMEM((2, ROWS, NHALF), jnp.int16),
            pltpu.VMEM((2, ROWS, NHALF), jnp.int16),
            pltpu.VMEM((2, 8, 128), f32),
            pltpu.VMEM((2, 8, 128), f32),
            pltpu.VMEM((NY, 2, ROWS), f32),
            pltpu.VMEM((4, 2, ROWS), f32),
            dma,
            dma((SUBS,)), dma((SUBS,)),
            dma((8 * SUBS,)), dma((8 * SUBS,)),
            dma((8 * SUBS,)), dma((8 * SUBS,)),
            dma((4 * SLOTS + 8,)), dma((2, len(PARTS), SLOTS)),
            dma((2,)), dma((2,)),
            dma((2,)), dma((2,)),
            dma((NY + 3,)), dma((NY + 3,)),
            pltpu.SemaphoreType.REGULAR((3,)),
        ],
        compiler_params=pltpu.CompilerParams(
            collective_id=0, has_side_effects=True, vmem_limit_bytes=60 * 2**20
        ),
        cost_estimate=pl.CostEstimate(flops=2 * ROWS * 2 * HALF * COLS, bytes_accessed=8 * 2**20, transcendentals=0),
        name="project_and_score",
    )(codes, offsets.T, responses, head)
    out, scores = pl.pallas_call(
        results,
        out_shape=(
            jax.ShapeDtypeStruct((ROWS, COLS), bf16),
            jax.ShapeDtypeStruct((1, ROWS), f32),
        ),
        name="results",
    )(out, scores)
    return out, scores.reshape(ROWS)


def solution(mesh):
    in_specs = (P("fsdp", "tp"), P("fsdp", "tp"), P("fsdp", None), P("tp"))
    out_specs = (P("fsdp", "tp"), P("fsdp"))
    return jax.shard_map(
        on_device, mesh=mesh, in_specs=in_specs, out_specs=out_specs, check_vma=False
    )
```

```python
import jax
import jax.numpy as jnp
from jax import lax
from jax.experimental import pallas as pl
from jax.experimental.pallas import tpu as pltpu
from jax.sharding import PartitionSpec as P

MESH = pl.DeviceIdType.MESH
BLK = 128
D = 8192
NX, NY, NZ, NH = 4, 8, 6, 3
ROWS = 256
CHUNK = 640
COLS = 256
NHALF = 128
HALF = NX * NH * CHUNK
SLOTS = NX * NH
ZF = 512
ZT, XT = (ZF // 2 + 15) // 16 * 16, ((CHUNK - ZF) // 2 + 15) // 16 * 16
PARTS = ((0, ZF), (0, ZT), (ZT, ZF - ZT), (ZF, CHUNK - ZF), (ZF, XT), (ZF + XT, CHUNK - ZF - XT))
ZALL, ZTOP, ZLOW, XALL, XTOP, XLOW = range(len(PARTS))
SUBS = 4
SUB = HALF // SUBS
PIECE = ROWS // (2 * NY)
PLANE = NX * CHUNK
ORDER = (
    ("z", 0, ZALL, "near"), ("rows", 3), ("x", 1, ZALL, 1), ("rows", 0),
    ("rows", 2), ("x", 0, ZALL, 3), ("x", 0, XALL, 3), ("x", 1, XALL, 3),
    ("x", 1, XALL, 1), ("start", 3), ("x", 0, ZALL, 1), ("x", 1, ZALL, 3),
    ("rows", 1), ("z", 0, ZALL, "far"), ("start", 0), ("pass", 1, ZALL, "own", 3),
    ("pass", 0, XALL, "own", 1), ("x", 0, XALL, 1), ("start", 2), ("ring", 1, 0, 1),
    ("ring", -1, 0, 1), ("ring", 1, 3, 1), ("z", 1, ZALL, "far"), ("pass", 0, ZALL, "own", 3),
    ("z", 1, ZALL, "near"), ("ring", -1, 3, 1), ("pass", 0, ZALL, "own", 1), ("turn_x", 0, "near"),
    ("turn_z", 0, 1), ("pass", 0, XALL, "own", 3), ("pass", 1, XALL, "own", 1), ("ring", 1, 0, 2),
    ("ring", -1, 0, 2), ("turn_z", 0, 0), ("start", 1), ("word_z",),
    ("ring", 1, 3, 2), ("turn_x", 0, "far"), ("ring", -1, 3, 2), ("ring", 1, 2, 1),
    ("ring", -1, 2, 1), ("turn_z", 0, 3), ("ring", 1, 1, 1), ("ring", -1, 1, 1),
    ("turn_x", 1, "near"), ("pass", 0, ZALL, "near", 1), ("turn_z", 0, 2), ("ring", 1, 2, 2),
    ("ring", -1, 2, 2), ("pass", 1, XALL, "own", 3), ("ring", 1, 1, 2), ("ring", -1, 1, 2),
    ("turn_z", 1, 0), ("ring", 1, 0, 3), ("pass", 0, ZALL, "far", 1), ("ring", -1, 3, 3),
    ("turn_x", 1, "far"), ("word_on",), ("ring", 1, 2, 3), ("turn_z", 1, 1),
    ("pass", 0, ZALL, "near", 3), ("ring", -1, 0, 3), ("pass", 1, ZALL, "own", 1), ("ring", -1, 1, 3),
    ("turn_z", 1, 3), ("ring", 1, 0, 4), ("ring", -1, 2, 3), ("pass", 1, ZALL, "near", 1),
    ("ring", -1, 3, 4), ("pass", 0, ZALL, "far", 3), ("ring", 1, 1, 3), ("pass", 1, ZALL, "near", 3),
    ("turn_z", 1, 2), ("ring", -1, 1, 4), ("ring", 1, 2, 4), ("pass", 1, ZALL, "far", 3),
    ("ring", 1, 3, 3), ("word_core",), ("partial", 0), ("pass", 1, ZALL, "far", 1),
    ("partial", 1),
)


def device(x, y, zl, zh, c):
    return (zl * NX + x, (zh * NY + y) * 2 + c)


def kernel(
    codes_in, offsets_in, responses, head_in, out, scores,
    codes, offsets, head, projected_out, in_sem, out_sem,
    rall, w, acc, pout, pin, kout, kin, ys, zs,
    own_sem, inj_s, inj_r, ring_s, ring_r, sib_s, sib_r,
    w_s, w_r, p_s, p_r, k_s, k_r, sc_s, sc_r, word,
):
    f, t = lax.axis_index("fsdp"), lax.axis_index("tp")
    x, zl = f % NX, f // NX
    c, y, zh = t % 2, (t // 2) % NY, t // (2 * NY)
    h, p = zl // NH, zl % NH

    sibling = device(x, y, zl, zh, 1 - c)

    def at_x(e):
        return device((x + e) % NX, y, zl, zh, c)

    def at_z(e):
        return device(x, y, h * NH + (p + e) % NH, zh, c)

    def at_y(e):
        return device(x, (y + e + NY) % NY, zl, zh, c)

    middle = (zl == NH - 1) | (zl == NH)
    mate_zl = jnp.where(middle, NZ - 1 - zl, (zl + 4) % 8)
    mate = device(x, y, mate_zl, zh, c)
    wants = device(x, y, mate_zl, jnp.where(middle, zh, 1 - zh), c)
    rest = [device(x, y, zl, (zh + g) % 2, (c + k) % 2) for g, k in ((0, 1), (1, 0), (1, 1))]

    barrier = pltpu.get_barrier_semaphore()
    partners = [sibling, wants, at_x(1), at_x(3), at_z(1), at_z(2), at_y(1), at_y(-1)]
    for partner in partners:
        pl.semaphore_signal(barrier, inc=1, device_id=partner, device_id_type=MESH)

    inputs = [
        pltpu.make_async_copy(src, dst, in_sem.at[n])
        for n, (src, dst) in enumerate(((codes_in, codes), (offsets_in, offsets), (head_in, head)))
    ]
    for copy in inputs:
        copy.start()
    own = pltpu.make_async_copy(
        responses.at[:, pl.ds(pl.multiple_of(h * HALF, 128), HALF)],
        rall.at[pl.ds(0, ROWS)],
        own_sem,
    )
    own.start()

    def slot(xe, pe):
        return ((p + pe) % NH) * NX + (x + xe) % NX

    mine = slot(0, 0)
    for copy in inputs:
        copy.wait()
    for i in range(CHUNK // BLK):
        for j in range(COLS // BLK):
            block = codes[i * BLK : (i + 1) * BLK, j * BLK : (j + 1) * BLK].astype(jnp.float32)
            amax = jnp.max(jnp.max(jnp.abs(block), axis=0, keepdims=True), axis=1, keepdims=True)
            scale = jnp.exp2(offsets[j : j + 1, i : i + 1].astype(jnp.float32)) / (amax + 1e-06)
            w[j, mine, i * BLK : (i + 1) * BLK] = (block * scale).astype(jnp.bfloat16)

    pl.semaphore_wait(barrier, len(partners))

    def tell(n, *to):
        for one in to:
            pl.semaphore_signal(word.at[n], inc=1, device_id=one, device_id_type=MESH)

    def hear(n, number):
        pl.semaphore_wait(word.at[n], number)

    sent = []

    def send(src, dst, send_sem, recv_sem, to):
        copy = pltpu.make_async_remote_copy(
            src_ref=src, dst_ref=dst, send_sem=send_sem, recv_sem=recv_sem,
            device_id=to, device_id_type=MESH,
        )
        copy.start()
        sent.append(copy)

    def arrived(dst, send_sem, recv_sem):
        pltpu.make_async_remote_copy(
            src_ref=dst, dst_ref=dst, send_sem=send_sem, recv_sem=recv_sem,
            device_id=sibling, device_id_type=MESH,
        ).wait_recv()

    def piece(yo, core, k):
        row = pl.multiple_of(ROWS + 2 * PIECE * yo + PIECE * core, PIECE)
        return rall.at[pl.ds(row, PIECE), pl.ds(k * SUB, SUB)]

    def part(n, kind, s):
        row, rows = PARTS[kind]
        return w.at[n, s, pl.ds(row, rows)]

    count = {"w": 0, "ring": 0}

    def send_w(n, kind, s, to):
        i = count["w"]
        count["w"] += 1
        send(part(n, kind, s), part(n, kind, s), w_s.at[i], w_r.at[n, kind, s], to)

    met = set()

    def arrived_w(n, kind, xe, plane):
        if (n, kind, xe, plane) not in met:
            met.add((n, kind, xe, plane))
            s = slot(xe, planes[plane])
            arrived(part(n, kind, s), w_s.at[0], w_r.at[n, kind, s])

    def send_rows(k):
        row = pl.multiple_of(2 * PIECE * y + PIECE * c, PIECE)
        col = pl.multiple_of((1 - h) * HALF + k * SUB, 128)
        send(
            responses.at[pl.ds(row, PIECE), pl.ds(col, SUB)],
            piece(y, c, k), inj_s.at[k], inj_r.at[k], wants,
        )

    near = jnp.where(p == NH - 1, 2, 1)
    far = NH - near

    planes = {"own": 0, "near": near, "far": far}
    sibs = []

    def steps(dir_, k):
        return 4 if (dir_ == 1) == (k % 2 == 0) else 3

    def ring(dir_, k, d):
        yo = (y - dir_ * d + NY) % NY
        ref = piece(yo, c, k)
        i = ((0 if dir_ == 1 else 1) * SUBS + k) * 4
        if d > 0:
            arrived(ref, ring_s.at[i + d - 1], ring_r.at[i + d - 1])
        if d < steps(dir_, k):
            send(ref, ref, ring_s.at[i + d], ring_r.at[i + d], at_y(dir_))
        if d > 0 or dir_ == 1:
            n = count["ring"]
            count["ring"] += 1
            send(ref, ref, sib_s.at[n], sib_r.at[n], sibling)
            sibs.append((yo, k, n))

    def ring_start(k):
        arrived(piece(y, c, k), inj_s.at[k], inj_r.at[k])
        ring(1, k, 0)
        ring(-1, k, 0)

    def start_x(n, kind, to):
        send_w(n, kind, mine, at_x(to))

    def start_z(n, kind, plane):
        send_w(n, kind, mine, at_z(planes[plane]))

    def pass_x(n, kind, plane, xe):
        arrived_w(n, kind, xe, plane)
        half = {(XALL, 1): XLOW, (XALL, 3): XTOP, (ZALL, 1): ZLOW, (ZALL, 3): ZTOP}[kind, xe]
        send_w(n, half, slot(xe, planes[plane]), at_x(NX - xe))

    def turn_z(n, xe):
        if xe:
            for kind in (XTOP, XLOW) if xe == 2 else (XALL,):
                arrived_w(n, kind, xe, "own")
        for plane in ("near", "far"):
            send_w(n, XALL, slot(xe, 0), at_z(planes[plane]))

    def turn_x(n, plane):
        arrived_w(n, ZALL, 0, plane)
        for to in (1, 3):
            send_w(n, ZALL, slot(0, planes[plane]), at_x(to))

    def whole_plane(n, plane):
        for xe in range(NX):
            if xe or plane != "own":
                for kind in (ZTOP, ZLOW) if xe == 2 else (ZALL,):
                    arrived_w(n, kind, xe, plane)
                for kind in (XTOP, XLOW) if xe == 2 and plane == "own" else (XALL,):
                    arrived_w(n, kind, xe, plane)

    def product(n, first, q):
        cols = pl.ds(pl.multiple_of(q * PLANE, 128), PLANE)
        weights = w[n, pl.ds(q * NX, NX)].reshape(PLANE, NHALF)
        return jnp.dot(rall[pl.ds(first, ROWS), cols], weights, preferred_element_type=jnp.float32)

    def partial(n):
        if n == 0:
            for yo, k, i in sibs:
                arrived(piece(yo, 1 - c, k), sib_s.at[i], sib_r.at[i])
        whole_plane(n, "own")
        sums = product(n, ROWS, p)
        for plane in ("near", "far"):
            whole_plane(n, plane)
            sums += product(n, ROWS, (p + planes[plane]) % NH)
        amax = jnp.max(jnp.max(jnp.abs(sums), axis=0, keepdims=True), axis=1, keepdims=True)
        unit = jnp.maximum(amax, 1e-30) / 32760.0
        pout[n] = jnp.floor(sums * (1.0 / unit) + 0.5).astype(jnp.int32).astype(jnp.int16)
        kout[n] = jnp.broadcast_to(unit, kout.shape[1:])
        send(pout.at[n], pin.at[n], p_s.at[n], p_r.at[n], mate)
        send(kout.at[n], kin.at[n], k_s.at[n], k_r.at[n], mate)

    def word_z():
        tell(0, at_z(1), at_z(2))

    def word_on():
        hear(0, 2)
        tell(1, wants)

    def word_core():
        hear(1, 1)
        tell(2, sibling)

    steps_of = {
        "rows": send_rows, "start": ring_start, "ring": ring, "x": start_x, "z": start_z,
        "pass": pass_x, "turn_z": turn_z, "turn_x": turn_x, "partial": partial,
        "word_z": word_z, "word_on": word_on, "word_core": word_core,
    }
    for name, *what in ORDER:
        steps_of[name](*what)

    hear(2, 1)
    own.wait()
    acc[...] = jnp.zeros_like(acc)

    def own_rows(i, carry):
        acc[i // NH] += product(i // NH, 0, i % NH)
        return carry

    lax.fori_loop(0, 2 * NH, own_rows, 0)
    for copy in sent[:-4]:
        copy.wait_send()
    del sent[:-4]
    halves = []
    for n in range(2):
        arrived(pin.at[n], p_s.at[n], p_r.at[n])
        arrived(kin.at[n], k_s.at[n], k_r.at[n])
        halves.append(acc[n] + pin[n].astype(jnp.int32).astype(jnp.float32) * kin[n, 0:1, 0:1])
        projected_out[:, n * NHALF : (n + 1) * NHALF] = halves[n].astype(out.dtype)
    result = pltpu.make_async_copy(projected_out, out, out_sem)
    result.start()

    def over_columns(v):
        return jnp.sum(v.T, axis=0, keepdims=True)

    heads = head[...].astype(jnp.float32).reshape(1, COLS)
    first, second = halves
    ys[y, 0:1] = over_columns(first * first + second * second)
    ys[y, 1:2] = over_columns(first * heads[:, :NHALF] + second * heads[:, NHALF:])
    for e in range(1, NY):
        send(ys.at[y], ys.at[y], sc_s.at[e], sc_r.at[e], at_y(e))
    for e in range(1, NY):
        arrived(ys.at[(y - e + NY) % NY], sc_s.at[e], sc_r.at[e])
    here = zh * 2 + c
    zs[here] = jnp.sum(ys[...], axis=0)
    for n, to in enumerate(rest):
        send(zs.at[here], zs.at[here], sc_s.at[NY + n], sc_r.at[NY + n], to)
    for n, (g, k) in enumerate(((0, 1), (1, 0), (1, 1))):
        arrived(zs.at[(zh + g) % 2 * 2 + (c + k) % 2], sc_s.at[NY + n], sc_r.at[NY + n])
    total = jnp.sum(zs[...], axis=0)
    scores[...] = total[1:2] / jnp.sqrt(total[0:1] / D + 1e-06)

    result.wait()
    for copy in sent:
        copy.wait_send()


def results(out_in, scores_in, out, scores):
    out[...] = out_in[...]
    scores[...] = scores_in[...]


def on_device(codes, offsets, responses, head):
    vmem = pl.BlockSpec(memory_space=pltpu.VMEM)
    hbm = pl.BlockSpec(memory_space=pl.ANY)
    dma = pltpu.SemaphoreType.DMA
    f32, bf16 = jnp.float32, jnp.bfloat16
    out, scores = pl.pallas_call(
        kernel,
        out_shape=(
            jax.ShapeDtypeStruct((ROWS, COLS), bf16),
            jax.ShapeDtypeStruct((1, ROWS), f32),
        ),
        in_specs=[hbm] * 4,
        out_specs=(hbm, vmem),
        scratch_shapes=[
            pltpu.VMEM((CHUNK, COLS), bf16),
            pltpu.VMEM((COLS // BLK, CHUNK // BLK), jnp.int32),
            pltpu.VMEM((COLS,), bf16),
            pltpu.VMEM((ROWS, COLS), bf16),
            dma((3,)), dma,
            pltpu.VMEM((2 * ROWS, HALF), bf16),
            pltpu.VMEM((2, SLOTS, CHUNK, NHALF), bf16),
            pltpu.VMEM((2, ROWS, NHALF), f32),
            pltpu.VMEM((2, ROWS, NHALF), jnp.int16),
            pltpu.VMEM((2, ROWS, NHALF), jnp.int16),
            pltpu.VMEM((2, 8, 128), f32),
            pltpu.VMEM((2, 8, 128), f32),
            pltpu.VMEM((NY, 2, ROWS), f32),
            pltpu.VMEM((4, 2, ROWS), f32),
            dma,
            dma((SUBS,)), dma((SUBS,)),
            dma((8 * SUBS,)), dma((8 * SUBS,)),
            dma((8 * SUBS,)), dma((8 * SUBS,)),
            dma((4 * SLOTS + 8,)), dma((2, len(PARTS), SLOTS)),
            dma((2,)), dma((2,)),
            dma((2,)), dma((2,)),
            dma((NY + 3,)), dma((NY + 3,)),
            pltpu.SemaphoreType.REGULAR((3,)),
        ],
        compiler_params=pltpu.CompilerParams(
            collective_id=0, has_side_effects=True, vmem_limit_bytes=60 * 2**20
        ),
        cost_estimate=pl.CostEstimate(flops=2 * ROWS * 2 * HALF * COLS, bytes_accessed=8 * 2**20, transcendentals=0),
        name="project_and_score",
    )(codes, offsets.T, responses, head)
    out, scores = pl.pallas_call(
        results,
        out_shape=(
            jax.ShapeDtypeStruct((ROWS, COLS), bf16),
            jax.ShapeDtypeStruct((1, ROWS), f32),
        ),
        name="results",
    )(out, scores)
    return out, scores.reshape(ROWS)


def solution(mesh):
    in_specs = (P("fsdp", "tp"), P("fsdp", "tp"), P("fsdp", None), P("tp"))
    out_specs = (P("fsdp", "tp"), P("fsdp"))
    return jax.shard_map(
        on_device, mesh=mesh, in_specs=in_specs, out_specs=out_specs, check_vma=False
    )
```
